512 devices in a mesh: seq: 64 (over x, z, core), tp: 8 (over y).
Axes of the slice: x: 4, y: 8, z: 8, core: 2. Of those that a mesh axis runs over, the one named last changes fastest.
Arguments:
- query: bfloat16 [65536, 4096], P(('seq', 'tp')), may hold values from -40 to 40, as said below
- keys: bfloat16 [65536, 1024], P(('seq', 'tp')), may hold values from -8 to 8
- values: bfloat16 [65536, 1024], P(('seq', 'tp')), may hold values from -12 to 12
- cotangent: bfloat16 [65536, 4096], P(('seq', 'tp')), may hold values from -158.39192 to 158.39192
- rate: float32 [128, 32], P('seq', 'tp'), may hold values from 0.0001171875 to 7, as said below
- gate_logit: float32 [32], P('tp'), may hold values from -2 to 2
Outputs:
- grad_query: bfloat16 [65536, 4096], P(('seq', 'tp'))
- grad_keys: bfloat16 [65536, 1024], P(('seq', 'tp'))
- grad_values: bfloat16 [65536, 1024], P(('seq', 'tp'))
The draws below stay inside these ranges and needn't reach their ends.
Inputs may be any that keep to these rules, and one draw needn't show every extreme that they name: `query`: in some draws a few queries are large multiples of earlier keys. `rate`: Positive.
All inputs are finite; a program needn't handle non-finite values.
Results may differ from the reference program's by a relative error of at most 0.0055.
Values may be sent and summed in bfloat16 or wider, within the bound.
No kernel may reach another device: no remote copies, remote signals or barrier semaphores. Data moves between devices by JAX's collectives and lax.ppermute only.
A program may use at most 128 MiB of HBM per device.

```python
import math
import jax
import jax.numpy as jnp
from jax import lax

FOCUS_CHANNELS = 32
KVH = 8
HD = 128
SEG = 512
STREAM_PORTIONS = 128
TOKENS = 65536


def base_keys(key):
    return jax.random.normal(jax.random.fold_in(key, 11), (TOKENS, KVH * HD), jnp.float32)


def query_field(key):
    return jax.random.normal(jax.random.fold_in(key, 13), (TOKENS, FOCUS_CHANNELS * HD), jnp.float32)


def draw_keys(key, part):
    return base_keys(key).astype(jnp.bfloat16)


def draw_query(key, part):
    return query_field(key).astype(jnp.bfloat16)


def draw_cotangent(key, part):
    shared = jnp.clip(query_field(key), -3.0, 3.0)
    own_key = jax.random.fold_in(key, 41)
    noise = jnp.clip(jax.random.normal(own_key, (TOKENS, FOCUS_CHANNELS * HD), jnp.float32), -6.0, 6.0)
    return (SEG ** 0.5 * (0.8 * noise + 0.6 * shared)).astype(jnp.bfloat16)


def draw_values(key, part):
    linked = 2.5 * base_keys(key)
    offsets = jax.random.normal(jax.random.fold_in(key, 21), (STREAM_PORTIONS, 1, KVH * HD), jnp.float32)
    token_part = jax.random.normal(jax.random.fold_in(key, 22), (STREAM_PORTIONS, SEG, KVH * HD), jnp.float32)
    mixed = (token_part + offsets).reshape(TOKENS, KVH * HD) + linked
    return jnp.clip(mixed, -12.0, 12.0).astype(jnp.bfloat16)


def draw_rate(key, part):
    upper_rate = 3.0
    channelwise_fading_speed = jnp.exp(jax.random.uniform(jax.random.fold_in(key, 31), (1, FOCUS_CHANNELS), jnp.float32, math.log(0.03 / STREAM_PORTIONS), math.log(upper_rate)))
    fading_multiplier = jnp.exp(jax.random.uniform(jax.random.fold_in(key, 32), (STREAM_PORTIONS, FOCUS_CHANNELS), jnp.float32, math.log(0.5), math.log(2.0)))
    clustered_bundles = jax.random.randint(jax.random.fold_in(key, 33), (STREAM_PORTIONS, FOCUS_CHANNELS), 0, 32) == 0
    discarded_fraction = jax.random.uniform(jax.random.fold_in(key, 34), (STREAM_PORTIONS, FOCUS_CHANNELS), jnp.float32, 0.2, 0.5)
    return channelwise_fading_speed * fading_multiplier + jnp.where(clustered_bundles, -jnp.log(1.0 - discarded_fraction), 0.0)


def level_of(stream_key, shape, pieces, smallest, high):
    def one(dim, shards_of):
        steps = jax.random.uniform(jax.random.fold_in(jax.random.fold_in(stream_key, 6), dim), (shards_of,), jnp.float32, smallest / len(pieces), high / len(pieces))
        return jnp.repeat(jnp.exp(steps), shape[dim] // shards_of).reshape((-1,) + (1,) * (len(shape) - dim - 1))

    loudness = one(*pieces[0])
    for cut in pieces[1:]:
        loudness = loudness * one(*cut)
    return loudness


def setup_inputs(seed: int = 0) -> dict:
    key_list = jax.random.split(jax.random.key(seed), 7)
    query = draw_query(jax.random.fold_in(key_list[6], 71), 0)
    keys = draw_keys(jax.random.fold_in(key_list[6], 71), 0)
    values = draw_values(jax.random.fold_in(key_list[6], 71), 0)
    cotangent = draw_cotangent(jax.random.fold_in(key_list[6], 71), 0)
    rate = draw_rate(jax.random.fold_in(key_list[6], 71), 0)
    gate_logit = jnp.clip(jax.random.uniform(key_list[5], (FOCUS_CHANNELS,), jnp.float32, -2.0, 2.0) * level_of(key_list[5], (FOCUS_CHANNELS,), ((0, 8),), -0.4, 0.0), -2.0, 2.0)
    return dict(query=query, keys=keys, values=values, cotangent=cotangent, rate=rate, gate_logit=gate_logit)


PRECISE = lax.Precision.HIGH

def feature_map(arg_value):
    return jnp.where(arg_value > 0, arg_value + 1.0, jnp.exp(jnp.minimum(arg_value, 0.0)))

def feature_slope(arg_value):
    return jnp.where(arg_value > 0, 1.0, jnp.exp(jnp.minimum(arg_value, 0.0)))

def local_grads(q_seg, k_seg, v_seg, d_seg):
    length, group_size, head_width = q_seg.shape
    row_count = group_size * length
    q_rows = jnp.transpose(q_seg, (1, 0, 2)).reshape(row_count, head_width)
    d_rows = jnp.transpose(d_seg, (1, 0, 2)).reshape(row_count, head_width)
    block_rows = min(512, row_count)
    score_scale = 1.0 / math.sqrt(head_width)
    key_pos = jnp.arange(length, dtype=jnp.int32)

    def advance(running, position):
        grad_k, grad_v = running
        offset = position * block_rows
        q_blk = lax.dynamic_slice_in_dim(q_rows, offset, block_rows, 0)
        d_blk = lax.dynamic_slice_in_dim(d_rows, offset, block_rows, 0)
        query_pos = (offset + jnp.arange(block_rows, dtype=jnp.int32)) % length
        visible = key_pos[None, :] <= query_pos[:, None]
        scores = jnp.dot(q_blk, k_seg.T, preferred_element_type=jnp.float32) * score_scale
        scores = jnp.where(visible, scores, -1e+30)
        row_max = lax.optimization_barrier(jnp.max(scores, axis=1, keepdims=True))
        weights = jnp.where(visible, jnp.exp(scores - row_max), 0.0)
        probs = weights / lax.optimization_barrier(jnp.sum(weights, axis=1, keepdims=True))
        probs_low = probs.astype(jnp.bfloat16)
        grad_p = jnp.dot(d_blk, v_seg.T, preferred_element_type=jnp.float32)
        row_inner = lax.optimization_barrier(jnp.sum(probs * grad_p, axis=1, keepdims=True))
        grad_s = (probs * (grad_p - row_inner) * score_scale).astype(jnp.bfloat16)
        grad_q = jnp.dot(grad_s, k_seg, preferred_element_type=jnp.float32)
        grad_k = grad_k + jnp.dot(grad_s.T, q_blk, preferred_element_type=jnp.float32)
        grad_v = grad_v + jnp.dot(probs_low.T, d_blk, preferred_element_type=jnp.float32)
        return ((grad_k, grad_v), grad_q)
    empty_grad = jnp.zeros((length, head_width), jnp.float32)
    (grad_k, grad_v), grad_q = lax.scan(advance, (empty_grad, empty_grad), jnp.arange(row_count // block_rows, dtype=jnp.int32))
    grad_q = jnp.transpose(grad_q.reshape(group_size, length, head_width), (1, 0, 2))
    return (grad_q, grad_k, grad_v)

def local_pack(head_inputs):
    return local_grads(head_inputs[0], head_inputs[1], head_inputs[2], head_inputs[3])

def memory_grads(q_seg, d_seg, memory, norm_sum, gates):
    queries32 = q_seg.astype(jnp.float32)
    features = feature_map(queries32)
    numer = jnp.einsum('thc,hcd->thd', features, memory, precision=PRECISE)
    denom = jnp.einsum('thc,hc->th', features, norm_sum, precision=PRECISE) + 1.0
    retrieved = numer / denom[:, :, None]
    mem_cot = gates[None, :, None] * d_seg.astype(jnp.float32)
    num_cot = mem_cot / denom[:, :, None]
    den_cot = -lax.optimization_barrier(jnp.sum(mem_cot * retrieved, axis=2)) / denom
    feat_cot = jnp.einsum('thd,hcd->thc', num_cot, memory, precision=PRECISE) + den_cot[:, :, None] * norm_sum[None]
    state_cot = jnp.einsum('thc,thd->hcd', features, num_cot, precision=PRECISE)
    norm_cot = jnp.einsum('thc,th->hc', features, den_cot, precision=PRECISE)
    return (feat_cot * feature_slope(queries32), state_cot, norm_cot)

def lookup_aggregate(seg_pair):
    features = feature_map(seg_pair[0].astype(jnp.float32))
    moments = jnp.einsum('tgc,tgd->gcd', features, seg_pair[1].astype(jnp.float32), precision=PRECISE)
    return (moments, lax.optimization_barrier(jnp.sum(features, axis=0)))

def key_grads(k_seg, v_seg, moment_grad, total_grad):
    keys32 = k_seg.astype(jnp.float32)
    features = feature_map(keys32)
    feat_cot = jnp.einsum('tgd,gcd->tgc', v_seg.astype(jnp.float32), moment_grad, precision=PRECISE) + total_grad[None]
    extra_v = jnp.einsum('tgc,gcd->tgd', features, moment_grad, precision=PRECISE)
    return (feat_cot * feature_slope(keys32), extra_v)

def finish_keys(seg_inputs):
    k_seg, v_seg, moment_grad, total_grad, grad_k, grad_v = seg_inputs
    extra_k, extra_v = key_grads(k_seg, v_seg, moment_grad, total_grad)
    return ((grad_k + extra_k).astype(jnp.bfloat16), (grad_v + extra_v).astype(jnp.bfloat16))

def segment_grads(q_seg, k_seg, v_seg, d_seg, memory, norm_sum, gates):
    seg_len, head_count, head_width = q_seg.shape
    kv_count = k_seg.shape[1]
    group_size = head_count // kv_count
    local_cot = ((1.0 - gates)[None, :, None] * d_seg.astype(jnp.float32)).astype(jnp.bfloat16)
    grad_q_mem, state_cot, norm_cot = memory_grads(q_seg, d_seg, memory, norm_sum, gates)
    q_groups = jnp.moveaxis(q_seg.reshape(seg_len, kv_count, group_size, head_width), 1, 0)
    c_groups = jnp.moveaxis(local_cot.reshape(seg_len, kv_count, group_size, head_width), 1, 0)
    grad_q, grad_k, grad_v = lax.map(local_pack, (q_groups, jnp.moveaxis(k_seg, 1, 0), jnp.moveaxis(v_seg, 1, 0), c_groups))
    grad_q = jnp.moveaxis(grad_q, 0, 1).reshape(seg_len, head_count, head_width) + grad_q_mem
    return (grad_q.astype(jnp.bfloat16), jnp.moveaxis(grad_k, 0, 1), jnp.moveaxis(grad_v, 0, 1), state_cot, norm_cot)

def chain_forward(start_state, moments, totals, decay, group_size):

    def advance(carried, seg_inputs):
        memory, norm_sum = carried
        moment, total_sum, fading_multiplier = seg_inputs
        next_memory = fading_multiplier[:, None, None] * memory + jnp.repeat(moment, group_size, axis=0)
        next_norm = fading_multiplier[:, None] * norm_sum + jnp.repeat(total_sum, group_size, axis=0)
        return ((next_memory, next_norm), (memory, norm_sum))
    return lax.scan(advance, start_state, (moments, totals, decay))

def chain_backward(start_state, state_cots, norm_cots, decay, kv_count):

    def retreat(carried, seg_inputs):
        state_next, norm_next = carried
        state_cot, norm_cot, fading_multiplier = seg_inputs
        head_count, head_width = norm_next.shape
        moment_grad = state_next.reshape(kv_count, head_count // kv_count, head_width, head_width).sum(axis=1)
        total_grad = norm_next.reshape(kv_count, head_count // kv_count, head_width).sum(axis=1)
        new_state = (state_cot + fading_multiplier[:, None, None] * state_next, norm_cot + fading_multiplier[:, None] * norm_next)
        return (new_state, (moment_grad, total_grad))
    return lax.scan(retreat, start_state, (state_cots, norm_cots, decay), reverse=True)

def reference(query, keys, values, cotangent, rate, gate_logit):
    group_size = FOCUS_CHANNELS // KVH
    q_all = query.reshape(STREAM_PORTIONS, SEG, FOCUS_CHANNELS, HD)
    k_all = keys.reshape(STREAM_PORTIONS, SEG, KVH, HD)
    v_all = values.reshape(STREAM_PORTIONS, SEG, KVH, HD)
    d_all = cotangent.reshape(STREAM_PORTIONS, SEG, FOCUS_CHANNELS, HD)
    gates = jax.nn.sigmoid(gate_logit)
    decay = jnp.exp(-rate)
    moments, totals = lax.map(lookup_aggregate, (k_all, v_all))
    empty_state = (jnp.zeros((FOCUS_CHANNELS, HD, HD), jnp.float32), jnp.zeros((FOCUS_CHANNELS, HD), jnp.float32))
    final_state, (states, norms) = chain_forward(empty_state, moments, totals, decay, group_size)

    def per_segment(seg_inputs):
        return segment_grads(seg_inputs[0], seg_inputs[1], seg_inputs[2], seg_inputs[3], seg_inputs[4], seg_inputs[5], gates)
    grad_query, resident_lookup_vectors, local_v, state_cots, norm_cots = lax.map(per_segment, (q_all, k_all, v_all, d_all, states, norms))
    first_state, (moment_grads, total_grads) = chain_backward(empty_state, state_cots, norm_cots, decay, KVH)
    grad_keys, grad_values = lax.map(finish_keys, (k_all, v_all, moment_grads, total_grads, resident_lookup_vectors, local_v))
    return (grad_query.reshape(TOKENS, FOCUS_CHANNELS * HD), grad_keys.reshape(TOKENS, KVH * HD), grad_values.reshape(TOKENS, KVH * HD))
```

```python
import functools
import math

import jax
import jax.numpy as jnp
from jax import lax
from jax.experimental import pallas as pl
from jax.experimental.pallas import tpu as pltpu
from jax.sharding import PartitionSpec as P

HD = 128
SEG = 512
HALF = 64
BLK = 256
F32 = jnp.float32
BF16 = jnp.bfloat16
SCALE = 1.0 / math.sqrt(HD)
LOG2E = 1.4426950408889634
EXACT = lax.Precision.HIGHEST
VMEM = pltpu.VMEM
SMEM = pltpu.SMEM
NN = (((1,), (0,)), ((), ()))
NT = (((1,), (1,)), ((), ()))
TN = (((0,), (0,)), ((), ()))


def mm(a, b, dims, precision=None):
    return lax.dot_general(a, b, dims, precision=precision, preferred_element_type=F32)


def split(a):
    hi = a.astype(BF16)
    return hi, (a - hi.astype(F32)).astype(BF16)


def mm3(a, b, dims):
    ah, al = a if isinstance(a, tuple) else split(a)
    bh, bl = b if isinstance(b, tuple) else split(b)
    return mm(ah, bh, dims) + (mm(al, bh, dims) + mm(ah, bl, dims))


def mm2(a, b, dims):
    ah, al = split(a)
    return mm(ah, b, dims) + mm(al, b, dims)


def features_of(x):
    slope = jnp.exp(jnp.minimum(x, 0.0))
    return slope + jnp.maximum(x, 0.0), slope


def params(mib):
    return pltpu.CompilerParams(vmem_limit_bytes=mib << 20)


def cost(flops, size, exps=0):
    return pl.CostEstimate(flops=flops, bytes_accessed=size, transcendentals=exps)


def moments_kernel(kv_ref, rate_ref, out_ref, moment_ref, total_ref):
    for e in range(2):
        rows = pl.ds(e * SEG, SEG)
        sk, _ = features_of(kv_ref[rows, :HD].astype(F32))
        moment = mm2(sk, kv_ref[rows, HD:], TN)
        total = jnp.sum(sk, axis=0, keepdims=True)
        out_ref[:, 2 * e, :] = moment[:HALF]
        out_ref[:, 2 * e + 1, :] = moment[HALF:]
        out_ref[:, 4 + e, :] = jnp.broadcast_to(total, (HALF, HD))
        if e == 0:
            moment_ref[...] = moment
            total_ref[...] = jnp.broadcast_to(total, (8, HD))
    out_ref[:, 6, :] = jnp.broadcast_to(rate_ref[...], (HALF, HD))
    out_ref[:, 7, :] = jnp.zeros((HALF, HD), F32)


def moments_call(kv, rate_row):
    return pl.pallas_call(
        moments_kernel,
        out_shape=(
            jax.ShapeDtypeStruct((HALF, 8, HD), F32),
            jax.ShapeDtypeStruct((HD, HD), F32),
            jax.ShapeDtypeStruct((8, HD), F32),
        ),
        compiler_params=params(16),
        cost_estimate=cost(2 * 2 * SEG * HD * HD * 2, 1 << 20, 2 * SEG * HD),
        name="moments",
    )(kv, rate_row)


def cumulative(rates):
    rows = lax.broadcasted_iota(jnp.int32, (HALF, HALF), 0)
    cols = lax.broadcasted_iota(jnp.int32, (HALF, HALF), 1)
    upto = (cols <= rows).astype(F32)
    before = (cols < rows).astype(F32)
    same = (cols == rows).astype(F32)
    upto_t = (rows <= cols).astype(F32)
    before_t = (rows < cols).astype(F32)
    return dict(
        inc_col=mm(upto, rates, NN, EXACT),
        exc_col=mm(before, rates, NN, EXACT),
        inc_row=mm(rates, upto_t, TN, EXACT),
        exc_row=mm(rates, before_t, TN, EXACT),
        row=mm(rates, same, TN, EXACT),
        rows=rows,
        cols=cols,
    )


def pair_col(a, h):
    return a[:, h : h + 1] + a[:, 4 + h : 5 + h]


def pair_row(a, h):
    return a[h : h + 1, :] + a[4 + h : 5 + h, :]


def forward_kernel(me_ref, in_ref, out_ref, norm_ref):
    c = cumulative(in_ref[:, 6, :])
    earlier = c["cols"] < c["rows"]
    x0 = jnp.concatenate([in_ref[:, 0, :], in_ref[:, 1, :], in_ref[:, 4, :]], axis=1)
    x1 = jnp.concatenate([in_ref[:, 2, :], in_ref[:, 3, :], in_ref[:, 5, :]], axis=1)
    mine = lax.broadcasted_iota(jnp.int32, (HALF, HD), 0) == me_ref[0]
    for h in range(4):
        gap = pair_col(c["exc_col"], h) - pair_row(c["inc_row"], h)
        second = jnp.exp(jnp.where(earlier, -gap, -1e30))
        first = second * jnp.exp(-c["row"][4 + h : 5 + h, :])
        state = mm(first, x0, NN, EXACT) + mm(second, x1, NN, EXACT)
        out_ref[:, 2 * h, :] = state[:, :HD]
        out_ref[:, 2 * h + 1, :] = state[:, HD : 2 * HD]
        own = jnp.sum(jnp.where(mine, state[:, 2 * HD :], 0.0), axis=0, keepdims=True)
        norm_ref[2 * h : 2 * h + 2, :] = jnp.broadcast_to(own, (2, HD))


def forward_call(me, recv):
    return pl.pallas_call(
        forward_kernel,
        in_specs=[pl.BlockSpec(memory_space=SMEM), pl.BlockSpec(memory_space=VMEM)],
        out_shape=(
            jax.ShapeDtypeStruct((HALF, 8, HD), F32),
            jax.ShapeDtypeStruct((8, HD), F32),
        ),
        compiler_params=params(16),
        cost_estimate=cost(4 * 2 * 64 * 128 * 384 * 6, 1 << 20, 4 * 8192),
        name="forward_scan",
    )(me, recv)


def attention_kernel(gate_ref, q_ref, d_ref, k_ref, v_ref, gq_ref, gk_ref, gv_ref):
    h = pl.program_id(1)
    rest = 1.0 - gate_ref[h]
    local_cot = (rest * d_ref[...].astype(F32)).astype(BF16)
    u_pos = lax.broadcasted_iota(jnp.int32, (BLK, BLK), 0)
    t_pos = lax.broadcasted_iota(jnp.int32, (BLK, BLK), 1)
    visible = u_pos <= t_pos
    nb = SEG // BLK
    ks = [k_ref[pl.ds(i * BLK, BLK), :] for i in range(nb)]
    vs = [v_ref[pl.ds(i * BLK, BLK), :] for i in range(nb)]
    grad_k = [None] * nb
    grad_v = [None] * nb

    def plus(a, b):
        return b if a is None else a + b

    for tb in range(nb):
        q = q_ref[pl.ds(tb * BLK, BLK), :]
        lc = local_cot[tb * BLK : (tb + 1) * BLK]
        s = [mm(ks[u], q, NT) for u in range(tb + 1)]
        s[tb] = jnp.where(visible, s[tb], -1e30)
        top = functools.reduce(jnp.maximum, [jnp.max(a, axis=0, keepdims=True) for a in s])
        w = [jnp.exp2((a - top) * (SCALE * LOG2E)) for a in s]
        total = sum(jnp.sum(a, axis=0, keepdims=True) for a in w)
        inv = 1.0 / total
        p = [a * inv for a in w]
        gp = [mm(vs[u], lc, NT) for u in range(tb + 1)]
        inner = sum(jnp.sum(a * b, axis=0, keepdims=True) for a, b in zip(p, gp))
        gs = [(a * (b - inner) * SCALE).astype(BF16) for a, b in zip(p, gp)]
        gq_t = None
        for u in range(tb + 1):
            gq_t = plus(gq_t, mm(ks[u], gs[u], TN))
            grad_k[u] = plus(grad_k[u], mm(gs[u], q, NN))
            grad_v[u] = plus(grad_v[u], mm(p[u].astype(BF16), lc, NN))
        gq_ref[pl.ds(tb * BLK, BLK), :] = gq_t.T

    @pl.when(h == 0)
    def _():
        for u in range(nb):
            gk_ref[pl.ds(u * BLK, BLK), :] = grad_k[u]
            gv_ref[pl.ds(u * BLK, BLK), :] = grad_v[u]

    @pl.when(h > 0)
    def _():
        for u in range(nb):
            gk_ref[pl.ds(u * BLK, BLK), :] += grad_k[u]
            gv_ref[pl.ds(u * BLK, BLK), :] += grad_v[u]


def attention_call(gates, q, d, kv):
    head = pl.BlockSpec((SEG, HD), lambda s, h: (s, h))
    return pl.pallas_call(
        attention_kernel,
        grid=(2, 4),
        in_specs=[
            pl.BlockSpec(memory_space=SMEM),
            head,
            head,
            pl.BlockSpec((SEG, HD), lambda s, h: (s, 0)),
            pl.BlockSpec((SEG, HD), lambda s, h: (s, 1)),
        ],
        out_specs=[
            head,
            pl.BlockSpec((SEG, HD), lambda s, h: (s, 0)),
            pl.BlockSpec((SEG, HD), lambda s, h: (s, 0)),
        ],
        out_shape=(
            jax.ShapeDtypeStruct((2 * SEG, 4 * HD), F32),
            jax.ShapeDtypeStruct((2 * SEG, HD), F32),
            jax.ShapeDtypeStruct((2 * SEG, HD), F32),
        ),
        compiler_params=params(32),
        cost_estimate=cost(8 * 5 * 2 * SEG * SEG * HD, 6 << 20, 8 * SEG * SEG),
        name="attention",
    )(gates, q, d, kv, kv)


def memory_kernel(
    gate_ref, rate_ref, q_ref, d_ref, local_ref, state_ref, norm_ref, moment_ref, total_ref,
    gq_ref, send_ref, later_ref, later_norm_ref, rows_ref,
):
    later = None
    later_norm = None
    for h in range(4):
        cols = pl.ds(h * HD, HD)
        gate = gate_ref[h]
        decay = jnp.exp(jnp.full((1, HD), -rate_ref[0, h], F32))
        memory = jnp.concatenate([state_ref[:, 2 * h, :], state_ref[:, 2 * h + 1, :]], axis=0)
        norm = norm_ref[2 * h : 2 * h + 1, :]
        cots = []
        for e in range(2):
            if e == 1:
                memory = decay * memory + moment_ref[...]
                norm = decay * norm + total_ref[0:1, :]
            rows = pl.ds(e * SEG, SEG)
            sq, slope = features_of(q_ref[rows, cols].astype(F32))
            sq_low = sq.astype(BF16)
            memory_low = memory.astype(BF16)
            numer = mm(sq_low, memory_low, NN)
            denom = jnp.sum(sq * norm, axis=1, keepdims=True) + 1.0
            inv = 1.0 / denom
            num_cot = (gate * d_ref[rows, cols].astype(F32)) * inv
            den_cot = -jnp.sum(num_cot * numer, axis=1, keepdims=True) * inv
            num_low = num_cot.astype(BF16)
            feat_cot = mm(num_low, memory_low, NT) + den_cot * norm
            gq_ref[rows, cols] = (local_ref[rows, cols] + feat_cot * slope).astype(BF16)
            cots.append((mm(sq_low, num_low, TN), jnp.sum(sq * den_cot, axis=0, keepdims=True)))
        own = cots[0][0] + decay * cots[1][0]
        own_norm = cots[0][1] + decay * cots[1][1]
        rows_ref[:, 2 * h, :] = own[:HALF]
        rows_ref[:, 2 * h + 1, :] = own[HALF:]
        upper = own_norm.astype(BF16).astype(F32)
        rows_ref[:, 8 + h, :] = jnp.broadcast_to(upper, (HALF, HD))
        rows_ref[:, 12 + h, :] = jnp.broadcast_to(own_norm - upper, (HALF, HD))
        later = cots[1][0] if later is None else later + cots[1][0]
        later_norm = cots[1][1] if later_norm is None else later_norm + cots[1][1]
    send_ref[...] = rows_ref[...].astype(BF16)
    later_ref[...] = later
    later_norm_ref[...] = jnp.broadcast_to(later_norm, (8, HD))


def memory_call(gates, rate, q, d, local, state, norm, moment, total):
    return pl.pallas_call(
        memory_kernel,
        in_specs=[pl.BlockSpec(memory_space=SMEM)] * 2 + [pl.BlockSpec(memory_space=VMEM)] * 7,
        out_shape=(
            jax.ShapeDtypeStruct((2 * SEG, 4 * HD), BF16),
            jax.ShapeDtypeStruct((HALF, 16, HD), BF16),
            jax.ShapeDtypeStruct((HD, HD), F32),
            jax.ShapeDtypeStruct((8, HD), F32),
        ),
        scratch_shapes=[pltpu.VMEM((HALF, 16, HD), F32)],
        compiler_params=params(32),
        cost_estimate=cost(8 * 3 * 2 * SEG * HD * HD, 6 << 20, 8 * SEG * HD),
        name="memory",
    )(gates, rate, q, d, local, state, norm, moment, total)


def backward_kernel(me_ref, first_ref, in_ref, out_ref, norm_ref, rows_ref):
    c = cumulative(first_ref[:, 6, :])
    rows_ref[...] = in_ref[...].astype(F32)
    after = c["cols"] > c["rows"]
    mine = lax.broadcasted_iota(jnp.int32, (HALF, HD), 0) == me_ref[0]
    one = zero = None
    for h in range(4):
        gap = pair_row(c["exc_row"], h) - pair_col(c["inc_col"], h)
        weight = jnp.exp(jnp.where(after, -gap, -1e30))
        own = jnp.concatenate(
            [
                rows_ref[:, 2 * h, :],
                rows_ref[:, 2 * h + 1, :],
                rows_ref[:, 8 + h, :] + rows_ref[:, 12 + h, :],
            ],
            axis=1,
        )
        carried = mm(weight, own, NN, EXACT)
        earlier = jnp.exp(-first_ref[:, 6, 4 + h : 5 + h]) * carried
        one = carried if one is None else one + carried
        zero = earlier if zero is None else zero + earlier
    for e, value in ((0, zero), (1, one)):
        out_ref[:, 2 * e, :] = value[:, :HD]
        out_ref[:, 2 * e + 1, :] = value[:, HD : 2 * HD]
        own = jnp.sum(jnp.where(mine, value[:, 2 * HD :], 0.0), axis=0, keepdims=True)
        norm_ref[4 * e : 4 * e + 4, :] = jnp.broadcast_to(own, (4, HD))


def backward_call(me, first, recv):
    return pl.pallas_call(
        backward_kernel,
        in_specs=[pl.BlockSpec(memory_space=SMEM)] + [pl.BlockSpec(memory_space=VMEM)] * 2,
        out_shape=(
            jax.ShapeDtypeStruct((HALF, 4, HD), F32),
            jax.ShapeDtypeStruct((8, HD), F32),
        ),
        scratch_shapes=[pltpu.VMEM((HALF, 16, HD), F32)],
        compiler_params=params(16),
        cost_estimate=cost(4 * 2 * 64 * 64 * 384 * 6, 1 << 20, 4 * 4096),
        name="backward_scan",
    )(me, first, recv)


def finish_kernel(kv_ref, cot_ref, norm_ref, later_ref, later_norm_ref, gk_ref, gv_ref, out_ref):
    for e in range(2):
        rows = pl.ds(e * SEG, SEG)
        moment_cot = jnp.concatenate([cot_ref[:, 2 * e, :], cot_ref[:, 2 * e + 1, :]], axis=0)
        total_cot = norm_ref[4 * e : 4 * e + 1, :]
        if e == 0:
            moment_cot = moment_cot + later_ref[...]
            total_cot = total_cot + later_norm_ref[0:1, :]
        sk, slope = features_of(kv_ref[rows, :HD].astype(F32))
        high, low = split(moment_cot)
        values = kv_ref[rows, HD:]
        feat_cot = mm(values, high, NT) + mm(values, low, NT) + total_cot
        extra_v = mm3(sk, (high, low), NN)
        out_ref[rows, :HD] = (gk_ref[rows, :] + feat_cot * slope).astype(BF16)
        out_ref[rows, HD:] = (gv_ref[rows, :] + extra_v).astype(BF16)


def finish_call(kv, cot, norm, later, later_norm, gk, gv):
    return pl.pallas_call(
        finish_kernel,
        out_shape=jax.ShapeDtypeStruct((2 * SEG, 2 * HD), BF16),
        compiler_params=params(16),
        cost_estimate=cost(2 * 5 * 2 * SEG * HD * HD, 3 << 20, 2 * SEG * HD),
        name="finish",
    )(kv, cot, norm, later, later_norm, gk, gv)


def to_heads(x, parts):
    tokens = x[0].shape[0]
    width = x[0].shape[1] // 8
    blocks = jnp.concatenate([a.reshape(tokens, 8, width) for a in x], axis=2)
    blocks = jnp.transpose(blocks, (1, 0, 2))
    moved = lax.all_to_all(blocks, "tp", split_axis=0, concat_axis=0, tiled=True)
    return moved.reshape(8 * tokens, parts * width)


def to_tokens(x):
    blocks = x.reshape(8, x.shape[0] // 8, x.shape[1])
    return lax.all_to_all(blocks, "tp", split_axis=0, concat_axis=0, tiled=True)


def over_seq(x):
    return lax.all_to_all(x, "seq", split_axis=0, concat_axis=0, tiled=True)


def local(query, keys, values, cotangent, rate, gate_logit):
    me = lax.axis_index("seq").astype(jnp.int32).reshape(1)
    gates = jax.nn.sigmoid(gate_logit)
    rate_row = jnp.pad(rate.reshape(1, 8), ((0, 0), (0, HD - 8)))
    kv = to_heads((keys, values), 2)
    q = to_heads((query,), 1)
    send, moment, total = moments_call(kv, rate_row)
    first = over_seq(send)
    d = to_heads((cotangent,), 1)
    states, norm = forward_call(me, first)
    state = over_seq(states)
    gq_local, gk, gv = attention_call(gates, q, d, kv)
    gq, cots, later, later_norm = memory_call(
        gates, rate, q, d, gq_local, state, norm, moment, total
    )
    third = over_seq(cots)
    gq_moved = to_tokens(gq)
    carried, carried_norm = backward_call(me, first, third)
    cot = over_seq(carried)
    gkv = finish_call(kv, cot, carried_norm, later, later_norm, gk, gv)
    gkv_moved = to_tokens(gkv)
    tokens = query.shape[0]
    grad_query = jnp.transpose(gq_moved, (1, 0, 2)).reshape(tokens, -1)
    grad_keys = jnp.transpose(gkv_moved[:, :, :HD], (1, 0, 2)).reshape(tokens, -1)
    grad_values = jnp.transpose(gkv_moved[:, :, HD:], (1, 0, 2)).reshape(tokens, -1)
    return grad_query, grad_keys, grad_values


def solution(mesh):
    rows = P(("seq", "tp"), None)
    in_specs = (rows, rows, rows, rows, P("seq", "tp"), P("tp"))
    return jax.shard_map(
        local, mesh=mesh, in_specs=in_specs, out_specs=(rows, rows, rows), check_vma=False
    )
```

```python
import functools
import math

import jax
import jax.numpy as jnp
from jax import lax
from jax.experimental import pallas as pl
from jax.experimental.pallas import tpu as pltpu
from jax.sharding import PartitionSpec as P

HD = 128
SEG = 512
HALF = 64
BLK = 256
F32 = jnp.float32
BF16 = jnp.bfloat16
SCALE = 1.0 / math.sqrt(HD)
LOG2E = 1.4426950408889634
EXACT = lax.Precision.HIGHEST
VMEM = pltpu.VMEM
SMEM = pltpu.SMEM
NN = (((1,), (0,)), ((), ()))
NT = (((1,), (1,)), ((), ()))
TN = (((0,), (0,)), ((), ()))


def mm(a, b, dims, precision=None):
    return lax.dot_general(a, b, dims, precision=precision, preferred_element_type=F32)


def split(a):
    hi = a.astype(BF16)
    return hi, (a - hi.astype(F32)).astype(BF16)


def mm3(a, b, dims):
    ah, al = a if isinstance(a, tuple) else split(a)
    bh, bl = b if isinstance(b, tuple) else split(b)
    return mm(ah, bh, dims) + (mm(al, bh, dims) + mm(ah, bl, dims))


def mm2(a, b, dims):
    ah, al = split(a)
    return mm(ah, b, dims) + mm(al, b, dims)


def features_of(x):
    slope = jnp.exp(jnp.minimum(x, 0.0))
    return slope + jnp.maximum(x, 0.0), slope


def params(mib):
    return pltpu.CompilerParams(vmem_limit_bytes=mib << 20)


def cost(flops, size, exps=0):
    return pl.CostEstimate(flops=flops, bytes_accessed=size, transcendentals=exps)


ROWS = 2 * HD + 16


def moments_kernel(kv_ref, rate_ref, out_ref):
    for e in range(2):
        rows = pl.ds(e * SEG, SEG)
        sk, _ = features_of(kv_ref[rows, :HD].astype(F32))
        out_ref[pl.ds(e * HD, HD), :] = mm2(sk, kv_ref[rows, HD:], TN)
        total = jnp.sum(sk, axis=0, keepdims=True)
        out_ref[pl.ds(2 * HD + 4 * e, 4), :] = jnp.broadcast_to(total, (4, HD))
    out_ref[pl.ds(2 * HD + 8, 8), :] = rate_ref[...]


def moments_call(kv, rate_rows):
    return pl.pallas_call(
        moments_kernel,
        out_shape=jax.ShapeDtypeStruct((ROWS, HD), F32),
        compiler_params=params(16),
        cost_estimate=cost(2 * 2 * SEG * HD * HD * 2, 1 << 20, 2 * SEG * HD),
        name="moments",
    )(kv, rate_rows)


def rate_row(ref, e, h):
    row = 2 * HD + 8 + 4 * e + h
    return ref[row : row + 1, :]


def term(ref, e):
    total = 2 * HD + 4 * e
    return ref[pl.ds(e * HD, HD), :], ref[total : total + 1, :]


def pack(send_ref, i, state, norm, decay):
    send_ref[pl.ds(i * HD, HD), :] = state.astype(BF16)
    return split_rows(norm), split_rows(decay)


def split_rows(a):
    upper = a.astype(BF16).astype(F32)
    return upper, a - upper


def pack_tail(send_ref, tails):
    (n0, d0), (n1, d1) = tails
    rows = [n0[0], n1[0], n0[1], n1[1], d0[0], d1[0], d0[1], d1[1]]
    tail = jnp.concatenate(rows + [jnp.zeros((8, HD), F32)], axis=0)
    send_ref[pl.ds(2 * HD, 16), :] = tail.astype(BF16)


def store_state(ref, i, state, norm, decay):
    ref[pl.ds(i * HD, HD), :] = state
    ref[2 * HD + i : 2 * HD + i + 1, :] = norm
    ref[2 * HD + 2 + i : 2 * HD + 3 + i, :] = decay


def load_state(ref, i):
    return (
        ref[pl.ds(i * HD, HD), :],
        ref[2 * HD + i : 2 * HD + i + 1, :],
        ref[2 * HD + 2 + i : 2 * HD + 3 + i, :],
    )


def chip_kernel(core_ref, own_ref, other_ref, base_ref, send_ref):
    is_first = core_ref[0] == 0

    def rate(ref, e, i):
        return jnp.where(is_first, rate_row(ref, e, i), rate_row(ref, e, 2 + i))

    tails = []
    for i in range(2):
        side = []
        for ref in (own_ref, other_ref):
            (m0, t0), (m1, t1) = term(ref, 0), term(ref, 1)
            fade = jnp.exp(-rate(ref, 1, i))
            both = jnp.exp(-(rate(ref, 0, i) + rate(ref, 1, i)))
            side.append((fade * m0 + m1, fade * t0 + t1, both))
        (m_own, t_own, a_own), (m_other, t_other, a_other) = side
        w_own = jnp.where(is_first, a_other, 1.0)
        w_other = jnp.where(is_first, 1.0, a_own)
        state = w_own * m_own + w_other * m_other
        norm = w_own * t_own + w_other * t_other
        decay = a_own * a_other
        store_state(base_ref, i, state, norm, decay)
        tails.append(pack(send_ref, i, state, norm, decay))
    base_ref[pl.ds(2 * HD + 4, 12), :] = jnp.zeros((12, HD), F32)
    pack_tail(send_ref, tails)


def chip_call(core, own, other):
    return pl.pallas_call(
        chip_kernel,
        in_specs=[pl.BlockSpec(memory_space=SMEM)] + [pl.BlockSpec(memory_space=VMEM)] * 2,
        out_shape=(
            jax.ShapeDtypeStruct((ROWS, HD), F32),
            jax.ShapeDtypeStruct((ROWS, HD), BF16),
        ),
        compiler_params=params(16),
        cost_estimate=cost(1 << 20, 1 << 19),
        name="chip_terms",
    )(core, own, other)


def round_kernel(start, recv_ref, base_ref, *refs):
    held_ref, out_ref, send_ref = (None,) * start + refs if start else refs
    tail = recv_ref[pl.ds(2 * HD, 16), :].astype(F32)
    tails = []
    for i in range(2):
        state = recv_ref[pl.ds(i * HD, HD), :].astype(F32)
        norm = tail[i : i + 1] + tail[2 + i : 3 + i]
        decay = tail[4 + i : 5 + i] + tail[6 + i : 7 + i]
        if not start:
            state0, norm0, decay0 = load_state(held_ref, i)
            state = state0 + decay0 * state
            norm = norm0 + decay0 * norm
            decay = decay0 * decay
        store_state(out_ref, i, state, norm, decay)
        state1, norm1, decay1 = load_state(base_ref, i)
        tails.append(
            pack(send_ref, i, state1 + decay1 * state, norm1 + decay1 * norm, decay1 * decay)
        )
    out_ref[pl.ds(2 * HD + 4, 12), :] = jnp.zeros((12, HD), F32)
    pack_tail(send_ref, tails)


def round_call(recv, base, held):
    start = held is None
    operands = (recv, base) if start else (recv, base, held)
    return pl.pallas_call(
        functools.partial(round_kernel, start),
        out_shape=(
            jax.ShapeDtypeStruct((ROWS, HD), F32),
            jax.ShapeDtypeStruct((ROWS, HD), BF16),
        ),
        compiler_params=params(16),
        cost_estimate=cost(1 << 20, 1 << 19),
        name="round",
    )(*operands)


def swap_cores(x):
    return lax.ppermute(x, "seq", [(i, i ^ 1) for i in range(lax.axis_size("seq"))])


def exclusive_scan(base, send, ahead):
    size = lax.axis_size("seq")
    held = None
    hop = 2
    while hop < size:
        moves = [(i, i + hop) if ahead else (i + hop, i) for i in range(size - hop)]
        held, send = round_call(lax.ppermute(send, "seq", moves), base, held)
        hop *= 2
    return held


def cumulative(rates):
    rows = lax.broadcasted_iota(jnp.int32, (HALF, HALF), 0)
    cols = lax.broadcasted_iota(jnp.int32, (HALF, HALF), 1)
    upto = (cols <= rows).astype(F32)
    before = (cols < rows).astype(F32)
    same = (cols == rows).astype(F32)
    upto_t = (rows <= cols).astype(F32)
    before_t = (rows < cols).astype(F32)
    return dict(
        inc_col=mm(upto, rates, NN, EXACT),
        exc_col=mm(before, rates, NN, EXACT),
        inc_row=mm(rates, upto_t, TN, EXACT),
        exc_row=mm(rates, before_t, TN, EXACT),
        row=mm(rates, same, TN, EXACT),
        rows=rows,
        cols=cols,
    )


def pair_col(a, h):
    return a[:, h : h + 1] + a[:, 4 + h : 5 + h]


def pair_row(a, h):
    return a[h : h + 1, :] + a[4 + h : 5 + h, :]


def attention_kernel(gate_ref, q_ref, d_ref, k_ref, v_ref, extra_ref, gq_ref, gk_ref, gv_ref):
    h = pl.program_id(1)
    rest = 1.0 - gate_ref[h]
    local_cot = (rest * d_ref[...].astype(F32)).astype(BF16)
    u_pos = lax.broadcasted_iota(jnp.int32, (BLK, BLK), 0)
    t_pos = lax.broadcasted_iota(jnp.int32, (BLK, BLK), 1)
    visible = u_pos <= t_pos
    nb = SEG // BLK
    ks = [k_ref[pl.ds(i * BLK, BLK), :] for i in range(nb)]
    vs = [v_ref[pl.ds(i * BLK, BLK), :] for i in range(nb)]
    grad_k = [None] * nb
    grad_v = [None] * nb

    def plus(a, b):
        return b if a is None else a + b

    for tb in range(nb):
        q = q_ref[pl.ds(tb * BLK, BLK), :]
        lc = local_cot[tb * BLK : (tb + 1) * BLK]
        s = [mm(ks[u], q, NT) for u in range(tb + 1)]
        s[tb] = jnp.where(visible, s[tb], -1e30)
        top = functools.reduce(jnp.maximum, [jnp.max(a, axis=0, keepdims=True) for a in s])
        w = [jnp.exp2((a - top) * (SCALE * LOG2E)) for a in s]
        total = sum(jnp.sum(a, axis=0, keepdims=True) for a in w)
        inv = 1.0 / total
        p = [a * inv for a in w]
        gp = [mm(vs[u], lc, NT) for u in range(tb + 1)]
        inner = sum(jnp.sum(a * b, axis=0, keepdims=True) for a, b in zip(p, gp))
        gs = [(a * (b - inner) * SCALE).astype(BF16) for a, b in zip(p, gp)]
        gq_t = None
        for u in range(tb + 1):
            gq_t = plus(gq_t, mm(ks[u], gs[u], TN))
            grad_k[u] = plus(grad_k[u], mm(gs[u], q, NN))
            grad_v[u] = plus(grad_v[u], mm(p[u].astype(BF16), lc, NN))
        rows = pl.ds(tb * BLK, BLK)
        gq_ref[rows, :] = (gq_t.T + extra_ref[rows, :]).astype(BF16)

    @pl.when(h == 0)
    def _():
        for u in range(nb):
            gk_ref[pl.ds(u * BLK, BLK), :] = grad_k[u]
            gv_ref[pl.ds(u * BLK, BLK), :] = grad_v[u]

    @pl.when(h > 0)
    def _():
        for u in range(nb):
            gk_ref[pl.ds(u * BLK, BLK), :] += grad_k[u]
            gv_ref[pl.ds(u * BLK, BLK), :] += grad_v[u]


def attention_call(gates, qd, kv, extra):
    head = pl.BlockSpec((SEG, HD), lambda s, h: (s, h))
    return pl.pallas_call(
        attention_kernel,
        grid=(2, 4),
        in_specs=[
            pl.BlockSpec(memory_space=SMEM),
            head,
            pl.BlockSpec((SEG, HD), lambda s, h: (s, 4 + h)),
            pl.BlockSpec((SEG, HD), lambda s, h: (s, 0)),
            pl.BlockSpec((SEG, HD), lambda s, h: (s, 1)),
            head,
        ],
        out_specs=[
            head,
            pl.BlockSpec((SEG, HD), lambda s, h: (s, 0)),
            pl.BlockSpec((SEG, HD), lambda s, h: (s, 0)),
        ],
        out_shape=(
            jax.ShapeDtypeStruct((2 * SEG, 6 * HD), BF16),
            jax.ShapeDtypeStruct((2 * SEG, HD), F32),
            jax.ShapeDtypeStruct((2 * SEG, HD), F32),
        ),
        compiler_params=params(32),
        cost_estimate=cost(8 * 5 * 2 * SEG * SEG * HD, 6 << 20, 8 * SEG * SEG),
        name="attention",
    )(gates, qd, qd, kv, kv, extra)


def memory_kernel(
    core_ref, gate_ref, qd_ref, own_ref, other_ref, held_ref, held_other_ref,
    extra_ref, send_ref, later_ref, later_norm_ref, rows_ref,
):
    later = None
    later_norm = None
    is_first = core_ref[0] == 0
    m0, t0 = term(other_ref, 0)
    m1, t1 = term(other_ref, 1)
    for h in range(4):
        cols = pl.ds(h * HD, HD)
        dcols = pl.ds((4 + h) * HD, HD)
        gate = gate_ref[h]
        here = is_first if h < 2 else jnp.logical_not(is_first)
        memory, norm, _ = (
            jnp.where(here, a, b)
            for a, b in zip(load_state(held_ref, h % 2), load_state(held_other_ref, h % 2))
        )
        fade = jnp.exp(-rate_row(other_ref, 1, h))
        both = jnp.exp(-(rate_row(other_ref, 0, h) + rate_row(other_ref, 1, h)))
        memory = jnp.where(is_first, memory, both * memory + (fade * m0 + m1))
        norm = jnp.where(is_first, norm, both * norm + (fade * t0 + t1))
        decay = jnp.exp(-rate_row(own_ref, 0, h))
        cots = []
        for e in range(2):
            if e == 1:
                moment, total = term(own_ref, 0)
                memory = decay * memory + moment
                norm = decay * norm + total
            rows = pl.ds(e * SEG, SEG)
            sq, slope = features_of(qd_ref[rows, cols].astype(F32))
            sq_low = sq.astype(BF16)
            memory_low = memory.astype(BF16)
            numer = mm(sq_low, memory_low, NN)
            denom = jnp.sum(sq * norm, axis=1, keepdims=True) + 1.0
            inv = 1.0 / denom
            num_cot = (gate * qd_ref[rows, dcols].astype(F32)) * inv
            den_cot = -jnp.sum(num_cot * numer, axis=1, keepdims=True) * inv
            num_low = num_cot.astype(BF16)
            feat_cot = mm(num_low, memory_low, NT) + den_cot * norm
            extra_ref[rows, cols] = feat_cot * slope
            cots.append((mm(sq_low, num_low, TN), jnp.sum(sq * den_cot, axis=0, keepdims=True)))
        own = cots[0][0] + decay * cots[1][0]
        own_norm = cots[0][1] + decay * cots[1][1]
        rows_ref[:, 2 * h, :] = own[:HALF]
        rows_ref[:, 2 * h + 1, :] = own[HALF:]
        rows_ref[:, 8 + h, :] = jnp.broadcast_to(own_norm, (HALF, HD))
        later = cots[1][0] if later is None else later + cots[1][0]
        later_norm = cots[1][1] if later_norm is None else later_norm + cots[1][1]
    lane = lax.broadcasted_iota(jnp.int32, (1, HD), 1)
    rest = jnp.zeros((1, HD), F32)
    for e in range(2):
        for h in range(4):
            rest = jnp.where(lane == 4 * e + h, rate_row(own_ref, e, h), rest)
    for part in range(4):
        upper, rest = split_rows(rest)
        rows_ref[:, 12 + part, :] = jnp.broadcast_to(upper, (HALF, HD))
    send_ref[...] = rows_ref[...].astype(BF16)
    later_ref[...] = later
    later_norm_ref[...] = jnp.broadcast_to(later_norm, (8, HD))


def memory_call(core, gates, qd, own, other, held, held_other):
    return pl.pallas_call(
        memory_kernel,
        in_specs=[pl.BlockSpec(memory_space=SMEM)] * 2 + [pl.BlockSpec(memory_space=VMEM)] * 5,
        out_shape=(
            jax.ShapeDtypeStruct((2 * SEG, 4 * HD), F32),
            jax.ShapeDtypeStruct((HALF, 16, HD), BF16),
            jax.ShapeDtypeStruct((HD, HD), F32),
            jax.ShapeDtypeStruct((8, HD), F32),
        ),
        scratch_shapes=[pltpu.VMEM((HALF, 16, HD), F32)],
        compiler_params=params(32),
        cost_estimate=cost(8 * 3 * 2 * SEG * HD * HD, 6 << 20, 8 * SEG * HD),
        name="memory",
    )(core, gates, qd, own, other, held, held_other)


def backward_kernel(me_ref, in_ref, out_ref, norm_ref, rows_ref):
    rows_ref[...] = in_ref[...].astype(F32)
    rates = sum(rows_ref[:, 12 + part, :] for part in range(3))
    c = cumulative(rates)
    after = c["cols"] > c["rows"]
    mine = lax.broadcasted_iota(jnp.int32, (HALF, HD), 0) == me_ref[0]
    one = zero = None
    for h in range(4):
        gap = pair_row(c["exc_row"], h) - pair_col(c["inc_col"], h)
        weight = jnp.exp(jnp.where(after, -gap, -1e30))
        own = jnp.concatenate(
            [rows_ref[:, 2 * h, :], rows_ref[:, 2 * h + 1, :], rows_ref[:, 8 + h, :]], axis=1
        )
        carried = mm(weight, own, NN, EXACT)
        earlier = jnp.exp(-rates[:, 4 + h : 5 + h]) * carried
        one = carried if one is None else one + carried
        zero = earlier if zero is None else zero + earlier
    for e, value in ((0, zero), (1, one)):
        out_ref[:, 2 * e, :] = value[:, :HD]
        out_ref[:, 2 * e + 1, :] = value[:, HD : 2 * HD]
        own = jnp.sum(jnp.where(mine, value[:, 2 * HD :], 0.0), axis=0, keepdims=True)
        norm_ref[4 * e : 4 * e + 4, :] = jnp.broadcast_to(own, (4, HD))


def backward_call(me, recv):
    return pl.pallas_call(
        backward_kernel,
        in_specs=[pl.BlockSpec(memory_space=SMEM)] + [pl.BlockSpec(memory_space=VMEM)],
        out_shape=(
            jax.ShapeDtypeStruct((HALF, 4, HD), F32),
            jax.ShapeDtypeStruct((8, HD), F32),
        ),
        scratch_shapes=[pltpu.VMEM((HALF, 16, HD), F32)],
        compiler_params=params(16),
        cost_estimate=cost(4 * 2 * 64 * 64 * 384 * 6, 1 << 20, 4 * 4096),
        name="backward_scan",
    )(me, recv)


def finish_kernel(
    grads_ref, kv_ref, cot_ref, norm_ref, later_ref, later_norm_ref, gk_ref, gv_ref, out_ref
):
    del grads_ref
    for e in range(2):
        rows = pl.ds(e * SEG, SEG)
        moment_cot = jnp.concatenate([cot_ref[:, 2 * e, :], cot_ref[:, 2 * e + 1, :]], axis=0)
        total_cot = norm_ref[4 * e : 4 * e + 1, :]
        if e == 0:
            moment_cot = moment_cot + later_ref[...]
            total_cot = total_cot + later_norm_ref[0:1, :]
        sk, slope = features_of(kv_ref[rows, :HD].astype(F32))
        high, low = split(moment_cot)
        values = kv_ref[rows, HD:]
        feat_cot = mm(values, high, NT) + mm(values, low, NT) + total_cot
        extra_v = mm3(sk, (high, low), NN)
        out_ref[rows, :HD] = (gk_ref[rows, :] + feat_cot * slope).astype(BF16)
        out_ref[rows, HD:] = (gv_ref[rows, :] + extra_v).astype(BF16)


def finish_call(grads, kv, cot, norm, later, later_norm, gk, gv):
    return pl.pallas_call(
        finish_kernel,
        grid=(1,),
        in_specs=[pl.BlockSpec(memory_space=pl.ANY)] + [pl.BlockSpec(memory_space=VMEM)] * 7,
        out_specs=pl.BlockSpec((2 * SEG, 2 * HD), lambda i: (0, 2)),
        out_shape=jax.ShapeDtypeStruct((2 * SEG, 6 * HD), BF16),
        input_output_aliases={0: 0},
        compiler_params=params(16),
        cost_estimate=cost(2 * 5 * 2 * SEG * HD * HD, 3 << 20, 2 * SEG * HD),
        name="finish",
    )(grads, kv, cot, norm, later, later_norm, gk, gv)


def to_heads(x, y):
    tokens, width = x.shape[0], x.shape[1] // 8
    blocks = jnp.concatenate([a.reshape(tokens, 8, width) for a in (x, y)], axis=2)
    blocks = jnp.transpose(blocks, (1, 0, 2))
    moved = lax.all_to_all(blocks, "tp", split_axis=0, concat_axis=0, tiled=True)
    return moved.reshape(8 * tokens, 2 * width)


def to_tokens(x):
    blocks = x.reshape(8, x.shape[0] // 8, x.shape[1])
    return lax.all_to_all(blocks, "tp", split_axis=0, concat_axis=0, tiled=True)


def columns(x, start, width):
    part = jnp.transpose(x[:, :, start : start + width], (1, 0, 2))
    return part.reshape(x.shape[1], -1)


def over_seq(x):
    return lax.all_to_all(x, "seq", split_axis=0, concat_axis=0, tiled=True)


def local(query, keys, values, cotangent, rate, gate_logit):
    me = lax.axis_index("seq").astype(jnp.int32).reshape(1)
    core = me % 2
    gates = jax.nn.sigmoid(gate_logit)
    rate_rows = jnp.broadcast_to(rate.reshape(8, 1), (8, HD))
    kv = to_heads(keys, values)
    qd = to_heads(query, cotangent)
    own = moments_call(kv, rate_rows)
    other = swap_cores(own)
    base, send = chip_call(core, own, other)
    held = exclusive_scan(base, send, True)
    held_other = swap_cores(held)
    extra, cots, later, later_norm = memory_call(core, gates, qd, own, other, held, held_other)
    third = over_seq(cots)
    grads, gk, gv = attention_call(gates, qd, kv, extra)
    carried, carried_norm = backward_call(me, third)
    cot = over_seq(carried)
    grads = finish_call(grads, kv, cot, carried_norm, later, later_norm, gk, gv)
    moved = to_tokens(grads)
    width = 4 * HD
    return (
        columns(moved, 0, width),
        columns(moved, width, HD),
        columns(moved, width + HD, HD),
    )


def solution(mesh):
    rows = P(("seq", "tp"), None)
    in_specs = (rows, rows, rows, rows, P("seq", "tp"), P("tp"))
    return jax.shard_map(
        local, mesh=mesh, in_specs=in_specs, out_specs=(rows, rows, rows), check_vma=False
    )
```

```python
import functools
import math

import jax
import jax.numpy as jnp
from jax import lax
from jax.experimental import pallas as pl
from jax.experimental.pallas import tpu as pltpu
from jax.sharding import PartitionSpec as P

HD = 128
SEG = 512
HALF = 64
BLK = 256
F32 = jnp.float32
BF16 = jnp.bfloat16
SCALE = 1.0 / math.sqrt(HD)
LOG2E = 1.4426950408889634
EXACT = lax.Precision.HIGHEST
VMEM = pltpu.VMEM
SMEM = pltpu.SMEM
NN = (((1,), (0,)), ((), ()))
NT = (((1,), (1,)), ((), ()))
TN = (((0,), (0,)), ((), ()))


def mm(a, b, dims, precision=None):
    return lax.dot_general(a, b, dims, precision=precision, preferred_element_type=F32)


def split(a):
    hi = a.astype(BF16)
    return hi, (a - hi.astype(F32)).astype(BF16)


def mm3(a, b, dims):
    ah, al = a if isinstance(a, tuple) else split(a)
    bh, bl = b if isinstance(b, tuple) else split(b)
    return mm(ah, bh, dims) + (mm(al, bh, dims) + mm(ah, bl, dims))


def mm2(a, b, dims):
    ah, al = split(a)
    return mm(ah, b, dims) + mm(al, b, dims)


def features_of(x):
    slope = jnp.exp(jnp.minimum(x, 0.0))
    return slope + jnp.maximum(x, 0.0), slope


def params(mib):
    return pltpu.CompilerParams(vmem_limit_bytes=mib << 20)


def cost(flops, size, exps=0):
    return pl.CostEstimate(flops=flops, bytes_accessed=size, transcendentals=exps)


ROWS = 2 * HD + 16


def moments_kernel(kv_ref, rate_ref, out_ref):
    for e in range(2):
        rows = pl.ds(e * SEG, SEG)
        sk, _ = features_of(kv_ref[rows, :HD].astype(F32))
        out_ref[pl.ds(e * HD, HD), :] = mm2(sk, kv_ref[rows, HD:], TN)
        total = jnp.sum(sk, axis=0, keepdims=True)
        out_ref[pl.ds(2 * HD + 4 * e, 4), :] = jnp.broadcast_to(total, (4, HD))
    out_ref[pl.ds(2 * HD + 8, 8), :] = rate_ref[...]


def moments_call(kv, rate_rows):
    return pl.pallas_call(
        moments_kernel,
        out_shape=jax.ShapeDtypeStruct((ROWS, HD), F32),
        compiler_params=params(16),
        cost_estimate=cost(2 * 2 * SEG * HD * HD * 2, 1 << 20, 2 * SEG * HD),
        name="moments",
    )(kv, rate_rows)


def rate_row(ref, e, h):
    row = 2 * HD + 8 + 4 * e + h
    return ref[row : row + 1, :]


def term(ref, e):
    total = 2 * HD + 4 * e
    return ref[pl.ds(e * HD, HD), :], ref[total : total + 1, :]


def pack(send_ref, i, state, norm, decay):
    send_ref[pl.ds(i * HD, HD), :] = state.astype(BF16)
    return split_rows(norm), split_rows(decay)


def split_rows(a):
    upper = a.astype(BF16).astype(F32)
    return upper, a - upper


def pack_tail(send_ref, tails):
    (n0, d0), (n1, d1) = tails
    rows = [n0[0], n1[0], n0[1], n1[1], d0[0], d1[0], d0[1], d1[1]]
    tail = jnp.concatenate(rows + [jnp.zeros((8, HD), F32)], axis=0)
    send_ref[pl.ds(2 * HD, 16), :] = tail.astype(BF16)


def store_state(ref, i, state, norm, decay):
    ref[pl.ds(i * HD, HD), :] = state
    ref[2 * HD + i : 2 * HD + i + 1, :] = norm
    ref[2 * HD + 2 + i : 2 * HD + 3 + i, :] = decay


def load_state(ref, i):
    return (
        ref[pl.ds(i * HD, HD), :],
        ref[2 * HD + i : 2 * HD + i + 1, :],
        ref[2 * HD + 2 + i : 2 * HD + 3 + i, :],
    )


def chip_kernel(core_ref, own_ref, other_ref, base_ref, send_ref):
    is_first = core_ref[0] == 0

    def rate(ref, e, i):
        return jnp.where(is_first, rate_row(ref, e, i), rate_row(ref, e, 2 + i))

    tails = []
    for i in range(2):
        side = []
        for ref in (own_ref, other_ref):
            (m0, t0), (m1, t1) = term(ref, 0), term(ref, 1)
            fade = jnp.exp(-rate(ref, 1, i))
            both = jnp.exp(-(rate(ref, 0, i) + rate(ref, 1, i)))
            side.append((fade * m0 + m1, fade * t0 + t1, both))
        (m_own, t_own, a_own), (m_other, t_other, a_other) = side
        w_own = jnp.where(is_first, a_other, 1.0)
        w_other = jnp.where(is_first, 1.0, a_own)
        state = w_own * m_own + w_other * m_other
        norm = w_own * t_own + w_other * t_other
        decay = a_own * a_other
        store_state(base_ref, i, state, norm, decay)
        tails.append(pack(send_ref, i, state, norm, decay))
    base_ref[pl.ds(2 * HD + 4, 12), :] = jnp.zeros((12, HD), F32)
    pack_tail(send_ref, tails)


def chip_call(core, own, other):
    return pl.pallas_call(
        chip_kernel,
        in_specs=[pl.BlockSpec(memory_space=SMEM)] + [pl.BlockSpec(memory_space=VMEM)] * 2,
        out_shape=(
            jax.ShapeDtypeStruct((ROWS, HD), F32),
            jax.ShapeDtypeStruct((ROWS, HD), BF16),
        ),
        compiler_params=params(16),
        cost_estimate=cost(1 << 20, 1 << 19),
        name="chip_terms",
    )(core, own, other)


def round_kernel(start, count, *refs):
    recv_refs, refs = refs[:count], refs[count:]
    base_ref = refs[0]
    held_ref = None if start else refs[1]
    out_ref, send_ref = refs[-2:]
    windows = [None, None] if start else [load_state(held_ref, i) for i in range(2)]
    for recv_ref in recv_refs:
        tail = recv_ref[pl.ds(2 * HD, 16), :].astype(F32)
        for i in range(2):
            state = recv_ref[pl.ds(i * HD, HD), :].astype(F32)
            norm = tail[i : i + 1] + tail[2 + i : 3 + i]
            decay = tail[4 + i : 5 + i] + tail[6 + i : 7 + i]
            if windows[i] is not None:
                state0, norm0, decay0 = windows[i]
                state = state0 + decay0 * state
                norm = norm0 + decay0 * norm
                decay = decay0 * decay
            windows[i] = (state, norm, decay)
    tails = []
    for i in range(2):
        state, norm, decay = windows[i]
        store_state(out_ref, i, state, norm, decay)
        state1, norm1, decay1 = load_state(base_ref, i)
        tails.append(
            pack(send_ref, i, state1 + decay1 * state, norm1 + decay1 * norm, decay1 * decay)
        )
    out_ref[pl.ds(2 * HD + 4, 12), :] = jnp.zeros((12, HD), F32)
    pack_tail(send_ref, tails)


def round_call(recv, base, held):
    operands = [*recv, base]
    if held is not None:
        operands.append(held)
    return pl.pallas_call(
        functools.partial(round_kernel, held is None, len(recv)),
        out_shape=(
            jax.ShapeDtypeStruct((ROWS, HD), F32),
            jax.ShapeDtypeStruct((ROWS, HD), BF16),
        ),
        compiler_params=params(16),
        cost_estimate=cost(1 << 20, 1 << 19),
        name="round",
    )(*operands)


def swap_cores(x):
    return lax.ppermute(x, "seq", [(i, i ^ 1) for i in range(lax.axis_size("seq"))])


def exclusive_scan(base, send, ahead):
    size = lax.axis_size("seq")
    held = None
    hop = 2
    while hop < size:
        radix = 2 if hop == 8 else 4
        recv = []
        for step in range(hop, min(radix * hop, size), hop):
            moves = [(i, i + step) if ahead else (i + step, i) for i in range(size - step)]
            recv.append(lax.ppermute(send, "seq", moves))
        held, send = round_call(recv, base, held)
        hop *= radix
    return held


def cumulative(rates):
    rows = lax.broadcasted_iota(jnp.int32, (HALF, HALF), 0)
    cols = lax.broadcasted_iota(jnp.int32, (HALF, HALF), 1)
    upto = (cols <= rows).astype(F32)
    before = (cols < rows).astype(F32)
    same = (cols == rows).astype(F32)
    upto_t = (rows <= cols).astype(F32)
    before_t = (rows < cols).astype(F32)
    return dict(
        inc_col=mm(upto, rates, NN, EXACT),
        exc_col=mm(before, rates, NN, EXACT),
        inc_row=mm(rates, upto_t, TN, EXACT),
        exc_row=mm(rates, before_t, TN, EXACT),
        row=mm(rates, same, TN, EXACT),
        rows=rows,
        cols=cols,
    )


def pair_col(a, h):
    return a[:, h : h + 1] + a[:, 4 + h : 5 + h]


def pair_row(a, h):
    return a[h : h + 1, :] + a[4 + h : 5 + h, :]


def retrieval_cots(gate, q, d, memory, norm):
    sq, slope = features_of(q.astype(F32))
    numer = mm(sq.astype(BF16), memory, NN)
    inv = 1.0 / (jnp.sum(sq * norm, axis=1, keepdims=True) + 1.0)
    num_cot = (gate * d.astype(F32)) * inv
    den_cot = -jnp.sum(num_cot * numer, axis=1, keepdims=True) * inv
    return sq, slope, num_cot, den_cot


def attention_kernel(
    gate_ref, q_ref, d_ref, k_ref, v_ref, memory_ref, norm_ref, *refs
):
    gq_ref, gk_ref, gv_ref, mark_ref = refs[-4:]
    mark_ref[...] = jnp.zeros_like(mark_ref)
    h = pl.program_id(0)
    memory, norm = memory_ref[...].astype(BF16), norm_ref[0:1, :]
    _, slope, num_cot, den_cot = retrieval_cots(
        gate_ref[h], q_ref[...], d_ref[...], memory, norm
    )
    extra = (mm(num_cot.astype(BF16), memory, NT) + den_cot * norm) * slope
    rest = 1.0 - gate_ref[h]
    local_cot = (rest * d_ref[...].astype(F32)).astype(BF16)
    u_pos = lax.broadcasted_iota(jnp.int32, (BLK, BLK), 0)
    t_pos = lax.broadcasted_iota(jnp.int32, (BLK, BLK), 1)
    visible = u_pos <= t_pos
    nb = SEG // BLK
    ks = [k_ref[pl.ds(i * BLK, BLK), :] for i in range(nb)]
    vs = [v_ref[pl.ds(i * BLK, BLK), :] for i in range(nb)]
    grad_k = [None] * nb
    grad_v = [None] * nb

    def plus(a, b):
        return b if a is None else a + b

    for tb in range(nb):
        q = q_ref[pl.ds(tb * BLK, BLK), :]
        lc = local_cot[tb * BLK : (tb + 1) * BLK]
        s = [mm(ks[u], q, NT) for u in range(tb + 1)]
        s[tb] = jnp.where(visible, s[tb], -1e30)
        top = functools.reduce(jnp.maximum, [jnp.max(a, axis=0, keepdims=True) for a in s])
        w = [jnp.exp2((a - top) * (SCALE * LOG2E)) for a in s]
        total = sum(jnp.sum(a, axis=0, keepdims=True) for a in w)
        inv = 1.0 / total
        p = [a * inv for a in w]
        gp = [mm(vs[u], lc, NT) for u in range(tb + 1)]
        inner = sum(jnp.sum(a * b, axis=0, keepdims=True) for a, b in zip(p, gp))
        gs = [(a * (b - inner) * SCALE).astype(BF16) for a, b in zip(p, gp)]
        gq_t = None
        for u in range(tb + 1):
            gq_t = plus(gq_t, mm(ks[u], gs[u], TN))
            grad_k[u] = plus(grad_k[u], mm(gs[u], q, NN))
            grad_v[u] = plus(grad_v[u], mm(p[u].astype(BF16), lc, NN))
        rows = pl.ds(tb * BLK, BLK)
        gq_ref[rows, :] = (gq_t.T + extra[tb * BLK : (tb + 1) * BLK]).astype(BF16)

    @pl.when(h == 0)
    def _():
        for u in range(nb):
            gk_ref[pl.ds(u * BLK, BLK), :] = grad_k[u]
            gv_ref[pl.ds(u * BLK, BLK), :] = grad_v[u]

    @pl.when(h > 0)
    def _():
        for u in range(nb):
            gk_ref[pl.ds(u * BLK, BLK), :] += grad_k[u]
            gv_ref[pl.ds(u * BLK, BLK), :] += grad_v[u]


def attention_call(seg, gates, qd, kv, kept, earlier=()):
    def head(first):
        return pl.BlockSpec((SEG, HD), lambda h: (seg, first + h))

    def shared(col):
        return pl.BlockSpec((SEG, HD), lambda h: (seg, col))

    return pl.pallas_call(
        attention_kernel,
        grid=(4,),
        in_specs=[
            pl.BlockSpec(memory_space=SMEM),
            head(0),
            head(4),
            shared(0),
            shared(1),
            pl.BlockSpec((HD, HD), lambda h: (4 * seg + h, 0)),
            pl.BlockSpec((8, HD), lambda h: (9 * HD // 8 + 4 * seg + h, 0)),
        ]
        + [pl.BlockSpec(memory_space=pl.ANY)] * len(earlier),
        out_specs=[head(0), shared(0), shared(0), pl.BlockSpec((8, HD), lambda h: (0, 0))],
        out_shape=(
            jax.ShapeDtypeStruct((2 * SEG, 6 * HD), BF16),
            jax.ShapeDtypeStruct((2 * SEG, HD), F32),
            jax.ShapeDtypeStruct((2 * SEG, HD), F32),
            jax.ShapeDtypeStruct((8, HD), F32),
        ),
        input_output_aliases={7 + i: i for i in range(len(earlier))},
        compiler_params=params(60),
        cost_estimate=cost(4 * 5 * 2 * SEG * SEG * HD, 3 << 20, 4 * SEG * SEG),
        name="attention",
    )(gates, qd, qd, kv, kv, kept, kept, *earlier)


def memory_kernel(
    core_ref, gate_ref, qd_ref, own_ref, other_ref, held_ref, held_other_ref,
    kept_ref, send_ref, rows_ref,
):
    later = None
    later_norm = None
    is_first = core_ref[0] == 0
    m0, t0 = term(other_ref, 0)
    m1, t1 = term(other_ref, 1)
    for h in range(4):
        cols = pl.ds(h * HD, HD)
        dcols = pl.ds((4 + h) * HD, HD)
        gate = gate_ref[h]
        here = is_first if h < 2 else jnp.logical_not(is_first)
        memory, norm, _ = (
            jnp.where(here, a, b)
            for a, b in zip(load_state(held_ref, h % 2), load_state(held_other_ref, h % 2))
        )
        fade = jnp.exp(-rate_row(other_ref, 1, h))
        both = jnp.exp(-(rate_row(other_ref, 0, h) + rate_row(other_ref, 1, h)))
        memory = jnp.where(is_first, memory, both * memory + (fade * m0 + m1))
        norm = jnp.where(is_first, norm, both * norm + (fade * t0 + t1))
        decay = jnp.exp(-rate_row(own_ref, 0, h))
        cots = []
        for e in range(2):
            if e == 1:
                moment, total = term(own_ref, 0)
                memory = decay * memory + moment
                norm = decay * norm + total
            rows = pl.ds(e * SEG, SEG)
            memory_low = memory.astype(BF16)
            kept_ref[pl.ds((4 * e + h) * HD, HD), :] = memory
            kept_ref[pl.ds(9 * HD + (4 * e + h) * 8, 8), :] = jnp.broadcast_to(norm, (8, HD))
            sq, _, num_cot, den_cot = retrieval_cots(
                gate, qd_ref[rows, cols], qd_ref[rows, dcols], memory_low, norm
            )
            state_cot = mm(sq.astype(BF16), num_cot.astype(BF16), TN)
            cots.append((state_cot, jnp.sum(sq * den_cot, axis=0, keepdims=True)))
        own = cots[0][0] + decay * cots[1][0]
        own_norm = cots[0][1] + decay * cots[1][1]
        rows_ref[:, 2 * h, :] = own[:HALF]
        rows_ref[:, 2 * h + 1, :] = own[HALF:]
        rows_ref[:, 8 + h, :] = jnp.broadcast_to(own_norm, (HALF, HD))
        later = cots[1][0] if later is None else later + cots[1][0]
        later_norm = cots[1][1] if later_norm is None else later_norm + cots[1][1]
    lane = lax.broadcasted_iota(jnp.int32, (1, HD), 1)
    rest = jnp.zeros((1, HD), F32)
    for e in range(2):
        for h in range(4):
            rest = jnp.where(lane == 4 * e + h, rate_row(own_ref, e, h), rest)
    for part in range(4):
        upper, rest = split_rows(rest)
        rows_ref[:, 12 + part, :] = jnp.broadcast_to(upper, (HALF, HD))
    send_ref[...] = rows_ref[...].astype(BF16)
    kept_ref[pl.ds(8 * HD, HD), :] = later
    kept_ref[pl.ds(9 * HD + 64, 8), :] = jnp.broadcast_to(later_norm, (8, HD))


def memory_call(core, gates, qd, own, other, held, held_other):
    return pl.pallas_call(
        memory_kernel,
        in_specs=[pl.BlockSpec(memory_space=SMEM)] * 2 + [pl.BlockSpec(memory_space=VMEM)] * 5,
        out_shape=(
            jax.ShapeDtypeStruct((9 * HD + 72, HD), F32),
            jax.ShapeDtypeStruct((HALF, 16, HD), BF16),
        ),
        scratch_shapes=[pltpu.VMEM((HALF, 16, HD), F32)],
        compiler_params=params(24),
        cost_estimate=cost(8 * 2 * 2 * SEG * HD * HD, 3 << 20, 8 * SEG * HD),
        name="memory",
    )(core, gates, qd, own, other, held, held_other)


def backward_kernel(me_ref, in_ref, earlier_ref, out_ref, norm_ref, rows_ref):
    del earlier_ref
    rows_ref[...] = in_ref[...].astype(F32)
    rates = sum(rows_ref[:, 12 + part, :] for part in range(3))
    c = cumulative(rates)
    after = c["cols"] > c["rows"]
    mine = lax.broadcasted_iota(jnp.int32, (HALF, HD), 0) == me_ref[0]
    one = zero = None
    for h in range(4):
        gap = pair_row(c["exc_row"], h) - pair_col(c["inc_col"], h)
        weight = jnp.exp(jnp.where(after, -gap, -1e30))
        own = jnp.concatenate(
            [rows_ref[:, 2 * h, :], rows_ref[:, 2 * h + 1, :], rows_ref[:, 8 + h, :]], axis=1
        )
        carried = mm(weight, own, NN, EXACT)
        earlier = jnp.exp(-rates[:, 4 + h : 5 + h]) * carried
        one = carried if one is None else one + carried
        zero = earlier if zero is None else zero + earlier
    for e, value in ((0, zero), (1, one)):
        out_ref[:, 2 * e, :] = value[:, :HD]
        out_ref[:, 2 * e + 1, :] = value[:, HD : 2 * HD]
        own = jnp.sum(jnp.where(mine, value[:, 2 * HD :], 0.0), axis=0, keepdims=True)
        norm_ref[4 * e : 4 * e + 4, :] = jnp.broadcast_to(own, (4, HD))


def backward_call(me, recv, earlier):
    return pl.pallas_call(
        backward_kernel,
        in_specs=[pl.BlockSpec(memory_space=SMEM)] + [
            pl.BlockSpec(memory_space=VMEM),
            pl.BlockSpec(memory_space=pl.ANY),
        ],
        out_shape=(
            jax.ShapeDtypeStruct((HALF, 4, HD), F32),
            jax.ShapeDtypeStruct((8, HD), F32),
        ),
        scratch_shapes=[pltpu.VMEM((HALF, 16, HD), F32)],
        compiler_params=params(16),
        cost_estimate=cost(4 * 2 * 64 * 64 * 384 * 6, 1 << 20, 4 * 4096),
        name="backward_scan",
    )(me, recv, earlier)


def finish_kernel(
    grads_ref, kv_ref, cot_ref, norm_ref, later_ref, later_norm_ref, gk_ref, gv_ref, out_ref
):
    del grads_ref
    is_last = pl.program_id(0) == 1

    def rows(low, high):
        return jnp.where(is_last, high, low)

    moment_cot = jnp.concatenate(
        [
            rows(cot_ref[:, 0, :], cot_ref[:, 2, :]),
            rows(cot_ref[:, 1, :], cot_ref[:, 3, :]),
        ],
        axis=0,
    )
    moment_cot = moment_cot + rows(later_ref[...], 0.0)
    total_cot = rows(norm_ref[0:1, :] + later_norm_ref[0:1, :], norm_ref[4:5, :])
    sk, slope = features_of(kv_ref[:, :HD].astype(F32))
    high, low = split(moment_cot)
    values = kv_ref[:, HD:]
    feat_cot = mm(values, high, NT) + mm(values, low, NT) + total_cot
    extra_v = mm3(sk, (high, low), NN)
    out_ref[:, :HD] = (gk_ref[...] + feat_cot * slope).astype(BF16)
    out_ref[:, HD:] = (gv_ref[...] + extra_v).astype(BF16)


def finish_call(grads, kv, cot, norm, kept, gk, gv):
    part = pl.BlockSpec((SEG, HD), lambda e: (e, 0))
    return pl.pallas_call(
        finish_kernel,
        grid=(2,),
        in_specs=[
            pl.BlockSpec(memory_space=pl.ANY),
            pl.BlockSpec((SEG, 2 * HD), lambda e: (e, 0)),
            pl.BlockSpec((HALF, 4, HD), lambda e: (0, 0, 0)),
            pl.BlockSpec((8, HD), lambda e: (0, 0)),
            pl.BlockSpec((HD, HD), lambda e: (8, 0)),
            pl.BlockSpec((8, HD), lambda e: (9 * HD // 8 + 8, 0)),
            part,
            part,
        ],
        out_specs=pl.BlockSpec((SEG, 2 * HD), lambda e: (e, 2)),
        out_shape=jax.ShapeDtypeStruct((2 * SEG, 6 * HD), BF16),
        input_output_aliases={0: 0},
        compiler_params=params(60),
        cost_estimate=cost(2 * 5 * 2 * SEG * HD * HD, 3 << 20, 2 * SEG * HD),
        name="finish",
    )(grads, kv, cot, norm, kept, kept, gk, gv)


def copies_kernel(moves, count, *refs):
    refs, sems = refs[:count], refs[count]
    copies = [
        pltpu.make_async_copy(refs[a].at[src], refs[b].at[dst], sems.at[i])
        for i, (a, src, b, dst) in enumerate(moves)
    ]
    for copy in copies:
        copy.start()
    for copy in copies:
        copy.wait()


def copies_call(moves, arrays, outs, mib, name):
    return pl.pallas_call(
        functools.partial(copies_kernel, moves, len(arrays) + len(outs)),
        in_specs=[pl.BlockSpec(memory_space=VMEM)] * len(arrays),
        out_specs=[pl.BlockSpec(memory_space=pl.ANY)] * len(outs),
        out_shape=[jax.ShapeDtypeStruct(shape, BF16) for shape in outs],
        scratch_shapes=[pltpu.SemaphoreType.DMA((len(moves),))],
        compiler_params=params(mib),
        cost_estimate=cost(0, 4 * sum(math.prod(shape) for shape in outs)),
        name=name,
    )(*arrays)


def pack_pair(x, y):
    tokens, width = x.shape[0], x.shape[1] // 8
    every = slice(None)
    moves = [
        (a, (every, pl.ds(g * width, width)), 2, (g, every, pl.ds(a * width, width)))
        for g in range(8)
        for a in range(2)
    ]
    return copies_call(moves, (x, y), [(8, tokens, 2 * width)], 60, "pack_pair")[0]


def unpack_grads(x):
    tokens = x.shape[1]
    every = slice(None)
    widths = (4 * HD, HD, HD)
    starts = (0, 4 * HD, 5 * HD)
    moves = [
        (0, (g, every, pl.ds(start, width)), 1 + i, (every, pl.ds(g * width, width)))
        for g in range(8)
        for i, (start, width) in enumerate(zip(starts, widths))
    ]
    outs = [(tokens, 8 * width) for width in widths]
    return copies_call(moves, (x,), outs, 8, "unpack_grads")


def side_by_side(x, y):
    tokens, width = x.shape[0], x.shape[1] // 8
    blocks = jnp.concatenate([a.reshape(tokens, 8, width) for a in (x, y)], axis=2)
    return jnp.transpose(blocks, (1, 0, 2))


def to_heads(blocks):
    moved = lax.all_to_all(blocks, "tp", split_axis=0, concat_axis=0, tiled=True)
    return moved.reshape(-1, blocks.shape[2])


def to_tokens(x):
    blocks = x.reshape(8, x.shape[0] // 8, x.shape[1])
    return lax.all_to_all(blocks, "tp", split_axis=0, concat_axis=0, tiled=True)


def over_seq(x):
    return lax.all_to_all(x, "seq", split_axis=0, concat_axis=0, tiled=True)


def local(query, keys, values, cotangent, rate, gate_logit):
    me = lax.axis_index("seq").astype(jnp.int32).reshape(1)
    core = me % 2
    gates = jax.nn.sigmoid(gate_logit)
    rate_rows = jnp.broadcast_to(rate.reshape(8, 1), (8, HD))
    kv = to_heads(pack_pair(keys, values))
    qd = to_heads(side_by_side(query, cotangent))
    own = moments_call(kv, rate_rows)
    other = swap_cores(own)
    base, send = chip_call(core, own, other)
    held = exclusive_scan(base, send, True)
    held_other = swap_cores(held)
    kept, cots = memory_call(core, gates, qd, own, other, held, held_other)
    arrived = over_seq(cots)
    *part, mark = attention_call(0, gates, qd, kv, kept)
    carried, carried_norm = backward_call(me, arrived, mark)
    cot = over_seq(carried)
    grads, gk, gv, _ = attention_call(1, gates, qd, kv, kept, part)
    grads = finish_call(grads, kv, cot, carried_norm, kept, gk, gv)
    return tuple(unpack_grads(to_tokens(grads)))


def solution(mesh):
    rows = P(("seq", "tp"), None)
    in_specs = (rows, rows, rows, rows, P("seq", "tp"), P("tp"))
    return jax.shard_map(
        local, mesh=mesh, in_specs=in_specs, out_specs=(rows, rows, rows), check_vma=False
    )
```

```python
import functools
import math

import jax
import jax.numpy as jnp
from jax import lax
from jax.experimental import pallas as pl
from jax.experimental.pallas import tpu as pltpu
from jax.sharding import PartitionSpec as P

HD = 128
SEG = 512
HALF = 64
BLK = 256
F32 = jnp.float32
BF16 = jnp.bfloat16
SCALE = 1.0 / math.sqrt(HD)
LOG2E = 1.4426950408889634
EXACT = lax.Precision.HIGHEST
VMEM = pltpu.VMEM
SMEM = pltpu.SMEM
NN = (((1,), (0,)), ((), ()))
NT = (((1,), (1,)), ((), ()))
TN = (((0,), (0,)), ((), ()))


def mm(a, b, dims, precision=None):
    return lax.dot_general(a, b, dims, precision=precision, preferred_element_type=F32)


def split(a):
    hi = a.astype(BF16)
    return hi, (a - hi.astype(F32)).astype(BF16)


def mm3(a, b, dims):
    ah, al = a if isinstance(a, tuple) else split(a)
    bh, bl = b if isinstance(b, tuple) else split(b)
    return mm(ah, bh, dims) + (mm(al, bh, dims) + mm(ah, bl, dims))


def mm2(a, b, dims):
    ah, al = split(a)
    return mm(ah, b, dims) + mm(al, b, dims)


def features_of(x):
    slope = jnp.exp(jnp.minimum(x, 0.0))
    return slope + jnp.maximum(x, 0.0), slope


def params(mib):
    return pltpu.CompilerParams(vmem_limit_bytes=mib << 20)


def cost(flops, size, exps=0):
    return pl.CostEstimate(flops=flops, bytes_accessed=size, transcendentals=exps)


ROWS = 2 * HD + 16


def moments_kernel(kv_ref, rate_ref, out_ref):
    for e in range(2):
        rows = pl.ds(e * SEG, SEG)
        sk, _ = features_of(kv_ref[rows, :HD].astype(F32))
        out_ref[pl.ds(e * HD, HD), :] = mm2(sk, kv_ref[rows, HD:], TN)
        total = jnp.sum(sk, axis=0, keepdims=True)
        out_ref[pl.ds(2 * HD + 4 * e, 4), :] = jnp.broadcast_to(total, (4, HD))
    out_ref[pl.ds(2 * HD + 8, 8), :] = rate_ref[...]


def moments_call(kv, rate_rows):
    return pl.pallas_call(
        moments_kernel,
        out_shape=jax.ShapeDtypeStruct((ROWS, HD), F32),
        compiler_params=params(16),
        cost_estimate=cost(2 * 2 * SEG * HD * HD * 2, 1 << 20, 2 * SEG * HD),
        name="moments",
    )(kv, rate_rows)


def rate_row(ref, e, h):
    row = 2 * HD + 8 + 4 * e + h
    return ref[row : row + 1, :]


def term(ref, e):
    total = 2 * HD + 4 * e
    return ref[pl.ds(e * HD, HD), :], ref[total : total + 1, :]


def pack(send_ref, i, state, norm, decay):
    send_ref[pl.ds(i * HD, HD), :] = state.astype(BF16)
    return split_rows(norm), split_rows(decay)


def split_rows(a):
    upper = a.astype(BF16).astype(F32)
    return upper, a - upper


def pack_tail(send_ref, tails):
    (n0, d0), (n1, d1) = tails
    rows = [n0[0], n1[0], n0[1], n1[1], d0[0], d1[0], d0[1], d1[1]]
    tail = jnp.concatenate(rows + [jnp.zeros((8, HD), F32)], axis=0)
    send_ref[pl.ds(2 * HD, 16), :] = tail.astype(BF16)


def store_state(ref, i, state, norm, decay):
    ref[pl.ds(i * HD, HD), :] = state
    ref[2 * HD + i : 2 * HD + i + 1, :] = norm
    ref[2 * HD + 2 + i : 2 * HD + 3 + i, :] = decay


def load_state(ref, i):
    return (
        ref[pl.ds(i * HD, HD), :],
        ref[2 * HD + i : 2 * HD + i + 1, :],
        ref[2 * HD + 2 + i : 2 * HD + 3 + i, :],
    )


def chip_kernel(core_ref, own_ref, other_ref, base_ref, send_ref):
    is_first = core_ref[0] == 0

    def rate(ref, e, i):
        return jnp.where(is_first, rate_row(ref, e, i), rate_row(ref, e, 2 + i))

    tails = []
    for i in range(2):
        side = []
        for ref in (own_ref, other_ref):
            (m0, t0), (m1, t1) = term(ref, 0), term(ref, 1)
            fade = jnp.exp(-rate(ref, 1, i))
            both = jnp.exp(-(rate(ref, 0, i) + rate(ref, 1, i)))
            side.append((fade * m0 + m1, fade * t0 + t1, both))
        (m_own, t_own, a_own), (m_other, t_other, a_other) = side
        w_own = jnp.where(is_first, a_other, 1.0)
        w_other = jnp.where(is_first, 1.0, a_own)
        state = w_own * m_own + w_other * m_other
        norm = w_own * t_own + w_other * t_other
        decay = a_own * a_other
        store_state(base_ref, i, state, norm, decay)
        tails.append(pack(send_ref, i, state, norm, decay))
    base_ref[pl.ds(2 * HD + 4, 12), :] = jnp.zeros((12, HD), F32)
    pack_tail(send_ref, tails)


def chip_call(core, own, other):
    return pl.pallas_call(
        chip_kernel,
        in_specs=[pl.BlockSpec(memory_space=SMEM)] + [pl.BlockSpec(memory_space=VMEM)] * 2,
        out_shape=(
            jax.ShapeDtypeStruct((ROWS, HD), F32),
            jax.ShapeDtypeStruct((ROWS, HD), BF16),
        ),
        compiler_params=params(16),
        cost_estimate=cost(1 << 20, 1 << 19),
        name="chip_terms",
    )(core, own, other)


def round_kernel(start, count, *refs):
    recv_refs, refs = refs[:count], refs[count:]
    base_ref = refs[0]
    held_ref = None if start else refs[1]
    out_ref, send_ref = refs[-2:]
    windows = [None, None] if start else [load_state(held_ref, i) for i in range(2)]
    for recv_ref in recv_refs:
        tail = recv_ref[pl.ds(2 * HD, 16), :].astype(F32)
        for i in range(2):
            state = recv_ref[pl.ds(i * HD, HD), :].astype(F32)
            norm = tail[i : i + 1] + tail[2 + i : 3 + i]
            decay = tail[4 + i : 5 + i] + tail[6 + i : 7 + i]
            if windows[i] is not None:
                state0, norm0, decay0 = windows[i]
                state = state0 + decay0 * state
                norm = norm0 + decay0 * norm
                decay = decay0 * decay
            windows[i] = (state, norm, decay)
    tails = []
    for i in range(2):
        state, norm, decay = windows[i]
        store_state(out_ref, i, state, norm, decay)
        state1, norm1, decay1 = load_state(base_ref, i)
        tails.append(
            pack(send_ref, i, state1 + decay1 * state, norm1 + decay1 * norm, decay1 * decay)
        )
    out_ref[pl.ds(2 * HD + 4, 12), :] = jnp.zeros((12, HD), F32)
    pack_tail(send_ref, tails)


def round_call(recv, base, held):
    operands = [*recv, base]
    if held is not None:
        operands.append(held)
    return pl.pallas_call(
        functools.partial(round_kernel, held is None, len(recv)),
        out_shape=(
            jax.ShapeDtypeStruct((ROWS, HD), F32),
            jax.ShapeDtypeStruct((ROWS, HD), BF16),
        ),
        compiler_params=params(16),
        cost_estimate=cost(1 << 20, 1 << 19),
        name="round",
    )(*operands)


def swap_cores(x):
    return lax.ppermute(x, "seq", [(i, i ^ 1) for i in range(lax.axis_size("seq"))])


def exclusive_scan(base, send, ahead):
    size = lax.axis_size("seq")
    held = None
    hop = 2
    while hop < size:
        radix = 2 if hop == 8 else 4
        recv = []
        for step in range(hop, min(radix * hop, size), hop):
            moves = [(i, i + step) if ahead else (i + step, i) for i in range(size - step)]
            recv.append(lax.ppermute(send, "seq", moves))
        held, send = round_call(recv, base, held)
        hop *= radix
    return held


def cumulative(rates):
    rows = lax.broadcasted_iota(jnp.int32, (HALF, HALF), 0)
    cols = lax.broadcasted_iota(jnp.int32, (HALF, HALF), 1)
    upto = (cols <= rows).astype(F32)
    before = (cols < rows).astype(F32)
    same = (cols == rows).astype(F32)
    upto_t = (rows <= cols).astype(F32)
    before_t = (rows < cols).astype(F32)
    return dict(
        inc_col=mm(upto, rates, NN, EXACT),
        exc_col=mm(before, rates, NN, EXACT),
        inc_row=mm(rates, upto_t, TN, EXACT),
        exc_row=mm(rates, before_t, TN, EXACT),
        row=mm(rates, same, TN, EXACT),
        rows=rows,
        cols=cols,
    )


def pair_col(a, h):
    return a[:, h : h + 1] + a[:, 4 + h : 5 + h]


def pair_row(a, h):
    return a[h : h + 1, :] + a[4 + h : 5 + h, :]


def retrieval_cots(gate, q, d, memory, norm):
    sq, slope = features_of(q.astype(F32))
    numer = mm(sq.astype(BF16), memory, NN)
    inv = 1.0 / (jnp.sum(sq * norm, axis=1, keepdims=True) + 1.0)
    num_cot = (gate * d.astype(F32)) * inv
    den_cot = -jnp.sum(num_cot * numer, axis=1, keepdims=True) * inv
    return sq, slope, num_cot, den_cot


def attention_kernel(
    gate_ref, q_ref, d_ref, k_ref, v_ref, memory_ref, norm_ref, *refs
):
    gq_ref, gk_ref, gv_ref, mark_ref = refs[-4:]
    mark_ref[...] = jnp.zeros_like(mark_ref)
    h = pl.program_id(0)
    memory, norm = memory_ref[...].astype(BF16), norm_ref[0:1, :]
    _, slope, num_cot, den_cot = retrieval_cots(
        gate_ref[h], q_ref[...], d_ref[...], memory, norm
    )
    extra = (mm(num_cot.astype(BF16), memory, NT) + den_cot * norm) * slope
    rest = 1.0 - gate_ref[h]
    local_cot = (rest * d_ref[...].astype(F32)).astype(BF16)
    u_pos = lax.broadcasted_iota(jnp.int32, (BLK, BLK), 0)
    t_pos = lax.broadcasted_iota(jnp.int32, (BLK, BLK), 1)
    visible = u_pos <= t_pos
    nb = SEG // BLK
    ks = [k_ref[pl.ds(i * BLK, BLK), :] for i in range(nb)]
    vs = [v_ref[pl.ds(i * BLK, BLK), :] for i in range(nb)]
    grad_k = [None] * nb
    grad_v = [None] * nb

    def plus(a, b):
        return b if a is None else a + b

    for tb in range(nb):
        q = q_ref[pl.ds(tb * BLK, BLK), :]
        lc = local_cot[tb * BLK : (tb + 1) * BLK]
        s = [mm(ks[u], q, NT) for u in range(tb + 1)]
        s[tb] = jnp.where(visible, s[tb], -1e30)
        top = functools.reduce(jnp.maximum, [jnp.max(a, axis=0, keepdims=True) for a in s])
        w = [jnp.exp2((a - top) * (SCALE * LOG2E)) for a in s]
        total = sum(jnp.sum(a, axis=0, keepdims=True) for a in w)
        inv = 1.0 / total
        p = [a * inv for a in w]
        gp = [mm(vs[u], lc, NT) for u in range(tb + 1)]
        inner = sum(jnp.sum(a * b, axis=0, keepdims=True) for a, b in zip(p, gp))
        gs = [(a * (b - inner) * SCALE).astype(BF16) for a, b in zip(p, gp)]
        gq_t = None
        for u in range(tb + 1):
            gq_t = plus(gq_t, mm(ks[u], gs[u], TN))
            grad_k[u] = plus(grad_k[u], mm(gs[u], q, NN))
            grad_v[u] = plus(grad_v[u], mm(p[u].astype(BF16), lc, NN))
        rows = pl.ds(tb * BLK, BLK)
        gq_ref[rows, :] = (gq_t.T + extra[tb * BLK : (tb + 1) * BLK]).astype(BF16)

    @pl.when(h == 0)
    def _():
        for u in range(nb):
            gk_ref[pl.ds(u * BLK, BLK), :] = grad_k[u]
            gv_ref[pl.ds(u * BLK, BLK), :] = grad_v[u]

    @pl.when(h > 0)
    def _():
        for u in range(nb):
            gk_ref[pl.ds(u * BLK, BLK), :] += grad_k[u]
            gv_ref[pl.ds(u * BLK, BLK), :] += grad_v[u]


def attention_call(seg, gates, qd, kv, kept, earlier=()):
    def head(first):
        return pl.BlockSpec((SEG, HD), lambda h: (seg, first + h))

    def shared(col):
        return pl.BlockSpec((SEG, HD), lambda h: (seg, col))

    return pl.pallas_call(
        attention_kernel,
        grid=(4,),
        in_specs=[
            pl.BlockSpec(memory_space=SMEM),
            head(0),
            head(4),
            shared(0),
            shared(1),
            pl.BlockSpec((HD, HD), lambda h: (4 * seg + h, 0)),
            pl.BlockSpec((8, HD), lambda h: (9 * HD // 8 + 4 * seg + h, 0)),
        ]
        + [pl.BlockSpec(memory_space=pl.ANY)] * len(earlier),
        out_specs=[head(0), shared(0), shared(0), pl.BlockSpec((8, HD), lambda h: (0, 0))],
        out_shape=(
            jax.ShapeDtypeStruct((2 * SEG, 6 * HD), BF16),
            jax.ShapeDtypeStruct((2 * SEG, HD), F32),
            jax.ShapeDtypeStruct((2 * SEG, HD), F32),
            jax.ShapeDtypeStruct((8, HD), F32),
        ),
        input_output_aliases={7 + i: i for i in range(len(earlier))},
        compiler_params=params(60),
        cost_estimate=cost(4 * 5 * 2 * SEG * SEG * HD, 3 << 20, 4 * SEG * SEG),
        name="attention",
    )(gates, qd, qd, kv, kv, kept, kept, *earlier)


def memory_kernel(
    core_ref, gate_ref, qd_ref, own_ref, other_ref, held_ref, held_other_ref,
    kept_ref, send_ref, rows_ref,
):
    later = None
    later_norm = None
    is_first = core_ref[0] == 0
    m0, t0 = term(other_ref, 0)
    m1, t1 = term(other_ref, 1)
    for h in range(4):
        cols = pl.ds(h * HD, HD)
        dcols = pl.ds((4 + h) * HD, HD)
        gate = gate_ref[h]
        here = is_first if h < 2 else jnp.logical_not(is_first)
        memory, norm, _ = (
            jnp.where(here, a, b)
            for a, b in zip(load_state(held_ref, h % 2), load_state(held_other_ref, h % 2))
        )
        fade = jnp.exp(-rate_row(other_ref, 1, h))
        both = jnp.exp(-(rate_row(other_ref, 0, h) + rate_row(other_ref, 1, h)))
        memory = jnp.where(is_first, memory, both * memory + (fade * m0 + m1))
        norm = jnp.where(is_first, norm, both * norm + (fade * t0 + t1))
        decay = jnp.exp(-rate_row(own_ref, 0, h))
        cots = []
        for e in range(2):
            if e == 1:
                moment, total = term(own_ref, 0)
                memory = decay * memory + moment
                norm = decay * norm + total
            rows = pl.ds(e * SEG, SEG)
            memory_low = memory.astype(BF16)
            kept_ref[pl.ds((4 * e + h) * HD, HD), :] = memory
            kept_ref[pl.ds(9 * HD + (4 * e + h) * 8, 8), :] = jnp.broadcast_to(norm, (8, HD))
            sq, _, num_cot, den_cot = retrieval_cots(
                gate, qd_ref[rows, cols], qd_ref[rows, dcols], memory_low, norm
            )
            state_cot = mm(sq.astype(BF16), num_cot.astype(BF16), TN)
            cots.append((state_cot, jnp.sum(sq * den_cot, axis=0, keepdims=True)))
        own = cots[0][0] + decay * cots[1][0]
        own_norm = cots[0][1] + decay * cots[1][1]
        rows_ref[:, 2 * h, :] = own[:HALF]
        rows_ref[:, 2 * h + 1, :] = own[HALF:]
        rows_ref[:, 8 + h, :] = jnp.broadcast_to(own_norm, (HALF, HD))
        later = cots[1][0] if later is None else later + cots[1][0]
        later_norm = cots[1][1] if later_norm is None else later_norm + cots[1][1]
    lane = lax.broadcasted_iota(jnp.int32, (1, HD), 1)
    rest = jnp.zeros((1, HD), F32)
    for e in range(2):
        for h in range(4):
            rest = jnp.where(lane == 4 * e + h, rate_row(own_ref, e, h), rest)
    for part in range(4):
        upper, rest = split_rows(rest)
        rows_ref[:, 12 + part, :] = jnp.broadcast_to(upper, (HALF, HD))
    send_ref[...] = rows_ref[...].astype(BF16)
    kept_ref[pl.ds(8 * HD, HD), :] = later
    kept_ref[pl.ds(9 * HD + 64, 8), :] = jnp.broadcast_to(later_norm, (8, HD))


def memory_call(core, gates, qd, own, other, held, held_other):
    return pl.pallas_call(
        memory_kernel,
        in_specs=[pl.BlockSpec(memory_space=SMEM)] * 2 + [pl.BlockSpec(memory_space=VMEM)] * 5,
        out_shape=(
            jax.ShapeDtypeStruct((9 * HD + 72, HD), F32),
            jax.ShapeDtypeStruct((HALF, 16, HD), BF16),
        ),
        scratch_shapes=[pltpu.VMEM((HALF, 16, HD), F32)],
        compiler_params=params(24),
        cost_estimate=cost(8 * 2 * 2 * SEG * HD * HD, 3 << 20, 8 * SEG * HD),
        name="memory",
    )(core, gates, qd, own, other, held, held_other)


def backward_kernel(me_ref, in_ref, earlier_ref, out_ref, norm_ref, rows_ref):
    del earlier_ref
    rows_ref[...] = in_ref[...].astype(F32)
    rates = sum(rows_ref[:, 12 + part, :] for part in range(3))
    c = cumulative(rates)
    after = c["cols"] > c["rows"]
    mine = lax.broadcasted_iota(jnp.int32, (HALF, HD), 0) == me_ref[0]
    one = zero = None
    for h in range(4):
        gap = pair_row(c["exc_row"], h) - pair_col(c["inc_col"], h)
        weight = jnp.exp(jnp.where(after, -gap, -1e30))
        own = jnp.concatenate(
            [rows_ref[:, 2 * h, :], rows_ref[:, 2 * h + 1, :], rows_ref[:, 8 + h, :]], axis=1
        )
        carried = mm(weight, own, NN, EXACT)
        earlier = jnp.exp(-rates[:, 4 + h : 5 + h]) * carried
        one = carried if one is None else one + carried
        zero = earlier if zero is None else zero + earlier
    for e, value in ((0, zero), (1, one)):
        out_ref[:, 2 * e, :] = value[:, :HD]
        out_ref[:, 2 * e + 1, :] = value[:, HD : 2 * HD]
        own = jnp.sum(jnp.where(mine, value[:, 2 * HD :], 0.0), axis=0, keepdims=True)
        norm_ref[4 * e : 4 * e + 4, :] = jnp.broadcast_to(own, (4, HD))


def backward_call(me, recv, earlier):
    return pl.pallas_call(
        backward_kernel,
        in_specs=[pl.BlockSpec(memory_space=SMEM)] + [
            pl.BlockSpec(memory_space=VMEM),
            pl.BlockSpec(memory_space=pl.ANY),
        ],
        out_shape=(
            jax.ShapeDtypeStruct((HALF, 4, HD), F32),
            jax.ShapeDtypeStruct((8, HD), F32),
        ),
        scratch_shapes=[pltpu.VMEM((HALF, 16, HD), F32)],
        compiler_params=params(16),
        cost_estimate=cost(4 * 2 * 64 * 64 * 384 * 6, 1 << 20, 4 * 4096),
        name="backward_scan",
    )(me, recv, earlier)


def finish_kernel(
    grads_ref, kv_ref, cot_ref, norm_ref, later_ref, later_norm_ref, gk_ref, gv_ref, out_ref
):
    del grads_ref
    is_last = pl.program_id(0) == 1

    def rows(low, high):
        return jnp.where(is_last, high, low)

    moment_cot = jnp.concatenate(
        [
            rows(cot_ref[:, 0, :], cot_ref[:, 2, :]),
            rows(cot_ref[:, 1, :], cot_ref[:, 3, :]),
        ],
        axis=0,
    )
    moment_cot = moment_cot + rows(later_ref[...], 0.0)
    total_cot = rows(norm_ref[0:1, :] + later_norm_ref[0:1, :], norm_ref[4:5, :])
    sk, slope = features_of(kv_ref[:, :HD].astype(F32))
    high, low = split(moment_cot)
    values = kv_ref[:, HD:]
    feat_cot = mm(values, high, NT) + mm(values, low, NT) + total_cot
    extra_v = mm3(sk, (high, low), NN)
    out_ref[:, :HD] = (gk_ref[...] + feat_cot * slope).astype(BF16)
    out_ref[:, HD:] = (gv_ref[...] + extra_v).astype(BF16)


def finish_call(grads, kv, cot, norm, kept, gk, gv):
    part = pl.BlockSpec((SEG, HD), lambda e: (e, 0))
    return pl.pallas_call(
        finish_kernel,
        grid=(2,),
        in_specs=[
            pl.BlockSpec(memory_space=pl.ANY),
            pl.BlockSpec((SEG, 2 * HD), lambda e: (e, 0)),
            pl.BlockSpec((HALF, 4, HD), lambda e: (0, 0, 0)),
            pl.BlockSpec((8, HD), lambda e: (0, 0)),
            pl.BlockSpec((HD, HD), lambda e: (8, 0)),
            pl.BlockSpec((8, HD), lambda e: (9 * HD // 8 + 8, 0)),
            part,
            part,
        ],
        out_specs=pl.BlockSpec((SEG, 2 * HD), lambda e: (e, 2)),
        out_shape=jax.ShapeDtypeStruct((2 * SEG, 6 * HD), BF16),
        input_output_aliases={0: 0},
        compiler_params=params(53),
        cost_estimate=cost(2 * 5 * 2 * SEG * HD * HD, 3 << 20, 2 * SEG * HD),
        name="finish",
    )(grads, kv, cot, norm, kept, kept, gk, gv)


def copies_kernel(moves, count, *refs):
    refs, sems = refs[:count], refs[count]
    copies = [
        pltpu.make_async_copy(refs[a].at[src], refs[b].at[dst], sems.at[i])
        for i, (a, src, b, dst) in enumerate(moves)
    ]
    for copy in copies:
        copy.start()
    for copy in copies:
        copy.wait()


def copies_call(moves, arrays, outs, mib, name):
    return pl.pallas_call(
        functools.partial(copies_kernel, moves, len(arrays) + len(outs)),
        in_specs=[pl.BlockSpec(memory_space=VMEM)] * len(arrays),
        out_specs=[pl.BlockSpec(memory_space=pl.ANY)] * len(outs),
        out_shape=[jax.ShapeDtypeStruct(shape, BF16) for shape in outs],
        scratch_shapes=[pltpu.SemaphoreType.DMA((len(moves),))],
        compiler_params=params(mib),
        cost_estimate=cost(0, 4 * sum(math.prod(shape) for shape in outs)),
        name=name,
    )(*arrays)


def pack_pair(x, y):
    tokens, width = x.shape[0], x.shape[1] // 8
    every = slice(None)
    moves = [
        (a, (every, pl.ds(g * width, width)), 2, (g, every, pl.ds(a * width, width)))
        for g in range(8)
        for a in range(2)
    ]
    return copies_call(moves, (x, y), [(8, tokens, 2 * width)], 60, "pack_pair")[0]


def unpack_grads(x):
    tokens = x.shape[1]
    every = slice(None)
    widths = (4 * HD, HD, HD)
    starts = (0, 4 * HD, 5 * HD)
    moves = [
        (0, (g, every, pl.ds(start, width)), 1 + i, (every, pl.ds(g * width, width)))
        for g in range(8)
        for i, (start, width) in enumerate(zip(starts, widths))
    ]
    outs = [(tokens, 8 * width) for width in widths]
    return copies_call(moves, (x,), outs, 8, "unpack_grads")


def side_by_side(x, y):
    tokens, width = x.shape[0], x.shape[1] // 8
    blocks = jnp.concatenate([a.reshape(tokens, 8, width) for a in (x, y)], axis=2)
    return jnp.transpose(blocks, (1, 0, 2))


def to_heads(blocks):
    moved = lax.all_to_all(blocks, "tp", split_axis=0, concat_axis=0, tiled=True)
    return moved.reshape(-1, blocks.shape[2])


def to_tokens(x):
    blocks = x.reshape(8, x.shape[0] // 8, x.shape[1])
    return lax.all_to_all(blocks, "tp", split_axis=0, concat_axis=0, tiled=True)


def over_seq(x):
    return lax.all_to_all(x, "seq", split_axis=0, concat_axis=0, tiled=True)


def local(query, keys, values, cotangent, rate, gate_logit):
    me = lax.axis_index("seq").astype(jnp.int32).reshape(1)
    core = me % 2
    gates = jax.nn.sigmoid(gate_logit)
    rate_rows = jnp.broadcast_to(rate.reshape(8, 1), (8, HD))
    kv = to_heads(pack_pair(keys, values))
    qd = to_heads(side_by_side(query, cotangent))
    own = moments_call(kv, rate_rows)
    other = swap_cores(own)
    base, send = chip_call(core, own, other)
    held = exclusive_scan(base, send, True)
    held_other = swap_cores(held)
    kept, cots = memory_call(core, gates, qd, own, other, held, held_other)
    arrived = over_seq(cots)
    *part, mark = attention_call(0, gates, qd, kv, kept)
    carried, carried_norm = backward_call(me, arrived, mark)
    cot = over_seq(carried)
    grads, gk, gv, _ = attention_call(1, gates, qd, kv, kept, part)
    grads = finish_call(grads, kv, cot, carried_norm, kept, gk, gv)
    return tuple(unpack_grads(to_tokens(grads)))


def solution(mesh):
    rows = P(("seq", "tp"), None)
    in_specs = (rows, rows, rows, rows, P("seq", "tp"), P("tp"))
    return jax.shard_map(
        local, mesh=mesh, in_specs=in_specs, out_specs=(rows, rows, rows), check_vma=False
    )
```

```python
import functools
import math

import jax
import jax.numpy as jnp
from jax import lax
from jax.experimental import pallas as pl
from jax.experimental.pallas import tpu as pltpu
from jax.sharding import PartitionSpec as P

HD = 128
SEG = 512
HALF = 64
BLK = 256
F32 = jnp.float32
BF16 = jnp.bfloat16
SCALE = 1.0 / math.sqrt(HD)
LOG2E = 1.4426950408889634
EXACT = lax.Precision.HIGHEST
VMEM = pltpu.VMEM
SMEM = pltpu.SMEM
NN = (((1,), (0,)), ((), ()))
NT = (((1,), (1,)), ((), ()))
TN = (((0,), (0,)), ((), ()))


def mm(a, b, dims, precision=None):
    return lax.dot_general(a, b, dims, precision=precision, preferred_element_type=F32)


def split(a):
    hi = a.astype(BF16)
    return hi, (a - hi.astype(F32)).astype(BF16)


def mm3(a, b, dims):
    ah, al = a if isinstance(a, tuple) else split(a)
    bh, bl = b if isinstance(b, tuple) else split(b)
    return mm(ah, bh, dims) + (mm(al, bh, dims) + mm(ah, bl, dims))


def mm2(a, b, dims):
    ah, al = split(a)
    return mm(ah, b, dims) + mm(al, b, dims)


def features_of(x):
    slope = jnp.exp(jnp.minimum(x, 0.0))
    return slope + jnp.maximum(x, 0.0), slope


def params(mib):
    return pltpu.CompilerParams(vmem_limit_bytes=mib << 20)


def cost(flops, size, exps=0):
    return pl.CostEstimate(flops=flops, bytes_accessed=size, transcendentals=exps)


ROWS = 2 * HD + 16


def moments_kernel(kv_ref, rate_ref, out_ref):
    for e in range(2):
        rows = pl.ds(e * SEG, SEG)
        sk, _ = features_of(kv_ref[rows, :HD].astype(F32))
        out_ref[pl.ds(e * HD, HD), :] = mm2(sk, kv_ref[rows, HD:], TN)
        total = jnp.sum(sk, axis=0, keepdims=True)
        out_ref[pl.ds(2 * HD + 4 * e, 4), :] = jnp.broadcast_to(total, (4, HD))
    out_ref[pl.ds(2 * HD + 8, 8), :] = rate_ref[...]


def moments_call(kv, rate_rows):
    return pl.pallas_call(
        moments_kernel,
        out_shape=jax.ShapeDtypeStruct((ROWS, HD), F32),
        compiler_params=params(16),
        cost_estimate=cost(2 * 2 * SEG * HD * HD * 2, 1 << 20, 2 * SEG * HD),
        name="moments",
    )(kv, rate_rows)


def rate_row(ref, e, h):
    row = 2 * HD + 8 + 4 * e + h
    return ref[row : row + 1, :]


def term(ref, e):
    total = 2 * HD + 4 * e
    return ref[pl.ds(e * HD, HD), :], ref[total : total + 1, :]


def pack(send_ref, i, state, norm, decay):
    send_ref[pl.ds(i * HD, HD), :] = state.astype(BF16)
    return split_rows(norm), split_rows(decay)


def split_rows(a):
    upper = a.astype(BF16).astype(F32)
    return upper, a - upper


def pack_tail(send_ref, tails):
    (n0, d0), (n1, d1) = tails
    rows = [n0[0], n1[0], n0[1], n1[1], d0[0], d1[0], d0[1], d1[1]]
    tail = jnp.concatenate(rows + [jnp.zeros((8, HD), F32)], axis=0)
    send_ref[pl.ds(2 * HD, 16), :] = tail.astype(BF16)


def store_state(ref, i, state, norm, decay):
    ref[pl.ds(i * HD, HD), :] = state
    ref[2 * HD + i : 2 * HD + i + 1, :] = norm
    ref[2 * HD + 2 + i : 2 * HD + 3 + i, :] = decay


def load_state(ref, i):
    return (
        ref[pl.ds(i * HD, HD), :],
        ref[2 * HD + i : 2 * HD + i + 1, :],
        ref[2 * HD + 2 + i : 2 * HD + 3 + i, :],
    )


def chip_kernel(core_ref, own_ref, other_ref, base_ref, send_ref):
    is_first = core_ref[0] == 0

    def rate(ref, e, i):
        return jnp.where(is_first, rate_row(ref, e, i), rate_row(ref, e, 2 + i))

    tails = []
    for i in range(2):
        side = []
        for ref in (own_ref, other_ref):
            (m0, t0), (m1, t1) = term(ref, 0), term(ref, 1)
            fade = jnp.exp(-rate(ref, 1, i))
            both = jnp.exp(-(rate(ref, 0, i) + rate(ref, 1, i)))
            side.append((fade * m0 + m1, fade * t0 + t1, both))
        (m_own, t_own, a_own), (m_other, t_other, a_other) = side
        w_own = jnp.where(is_first, a_other, 1.0)
        w_other = jnp.where(is_first, 1.0, a_own)
        state = w_own * m_own + w_other * m_other
        norm = w_own * t_own + w_other * t_other
        decay = a_own * a_other
        store_state(base_ref, i, state, norm, decay)
        tails.append(pack(send_ref, i, state, norm, decay))
    base_ref[pl.ds(2 * HD + 4, 12), :] = jnp.zeros((12, HD), F32)
    pack_tail(send_ref, tails)


def chip_call(core, own, other):
    return pl.pallas_call(
        chip_kernel,
        in_specs=[pl.BlockSpec(memory_space=SMEM)] + [pl.BlockSpec(memory_space=VMEM)] * 2,
        out_shape=(
            jax.ShapeDtypeStruct((ROWS, HD), F32),
            jax.ShapeDtypeStruct((ROWS, HD), BF16),
        ),
        compiler_params=params(16),
        cost_estimate=cost(1 << 20, 1 << 19),
        name="chip_terms",
    )(core, own, other)


def round_kernel(start, count, *refs):
    recv_refs, refs = refs[:count], refs[count:]
    base_ref = refs[0]
    held_ref = None if start else refs[1]
    out_ref, send_ref = refs[-2:]
    windows = [None, None] if start else [load_state(held_ref, i) for i in range(2)]
    for recv_ref in recv_refs:
        tail = recv_ref[pl.ds(2 * HD, 16), :].astype(F32)
        for i in range(2):
            state = recv_ref[pl.ds(i * HD, HD), :].astype(F32)
            norm = tail[i : i + 1] + tail[2 + i : 3 + i]
            decay = tail[4 + i : 5 + i] + tail[6 + i : 7 + i]
            if windows[i] is not None:
                state0, norm0, decay0 = windows[i]
                state = state0 + decay0 * state
                norm = norm0 + decay0 * norm
                decay = decay0 * decay
            windows[i] = (state, norm, decay)
    tails = []
    for i in range(2):
        state, norm, decay = windows[i]
        store_state(out_ref, i, state, norm, decay)
        state1, norm1, decay1 = load_state(base_ref, i)
        tails.append(
            pack(send_ref, i, state1 + decay1 * state, norm1 + decay1 * norm, decay1 * decay)
        )
    out_ref[pl.ds(2 * HD + 4, 12), :] = jnp.zeros((12, HD), F32)
    pack_tail(send_ref, tails)


def round_call(recv, base, held):
    operands = [*recv, base]
    if held is not None:
        operands.append(held)
    return pl.pallas_call(
        functools.partial(round_kernel, held is None, len(recv)),
        out_shape=(
            jax.ShapeDtypeStruct((ROWS, HD), F32),
            jax.ShapeDtypeStruct((ROWS, HD), BF16),
        ),
        compiler_params=params(16),
        cost_estimate=cost(1 << 20, 1 << 19),
        name="round",
    )(*operands)


def swap_cores(x):
    return lax.ppermute(x, "seq", [(i, i ^ 1) for i in range(lax.axis_size("seq"))])


def exclusive_scan(base, send, ahead):
    size = lax.axis_size("seq")
    held = None
    hop = 2
    while hop < size:
        radix = 2 if hop == 8 else 4
        recv = []
        for step in range(hop, min(radix * hop, size), hop):
            moves = [(i, i + step) if ahead else (i + step, i) for i in range(size - step)]
            recv.append(lax.ppermute(send, "seq", moves))
        held, send = round_call(recv, base, held)
        hop *= radix
    return held


def cumulative(rates):
    rows = lax.broadcasted_iota(jnp.int32, (HALF, HALF), 0)
    cols = lax.broadcasted_iota(jnp.int32, (HALF, HALF), 1)
    upto = (cols <= rows).astype(F32)
    before = (cols < rows).astype(F32)
    same = (cols == rows).astype(F32)
    upto_t = (rows <= cols).astype(F32)
    before_t = (rows < cols).astype(F32)
    return dict(
        inc_col=mm(upto, rates, NN, EXACT),
        exc_col=mm(before, rates, NN, EXACT),
        inc_row=mm(rates, upto_t, TN, EXACT),
        exc_row=mm(rates, before_t, TN, EXACT),
        row=mm(rates, same, TN, EXACT),
        rows=rows,
        cols=cols,
    )


def pair_col(a, h):
    return a[:, h : h + 1] + a[:, 4 + h : 5 + h]


def pair_row(a, h):
    return a[h : h + 1, :] + a[4 + h : 5 + h, :]


def retrieval_cots(gate, q, d, memory, norm):
    sq, slope = features_of(q.astype(F32))
    numer = mm(sq.astype(BF16), memory, NN)
    inv = 1.0 / (jnp.sum(sq * norm, axis=1, keepdims=True) + 1.0)
    num_cot = (gate * d.astype(F32)) * inv
    den_cot = -jnp.sum(num_cot * numer, axis=1, keepdims=True) * inv
    return sq, slope, num_cot, den_cot


def attention_kernel(
    gate_ref, q_ref, d_ref, k_ref, v_ref, memory_ref, norm_ref, *refs
):
    gq_ref, gk_ref, gv_ref, mark_ref = refs[-4:]
    mark_ref[...] = jnp.zeros_like(mark_ref)
    h = pl.program_id(0)
    memory, norm = memory_ref[...].astype(BF16), norm_ref[0:1, :]
    _, slope, num_cot, den_cot = retrieval_cots(
        gate_ref[h], q_ref[...], d_ref[...], memory, norm
    )
    extra = (mm(num_cot.astype(BF16), memory, NT) + den_cot * norm) * slope
    rest = 1.0 - gate_ref[h]
    local_cot = (rest * d_ref[...].astype(F32)).astype(BF16)
    u_pos = lax.broadcasted_iota(jnp.int32, (BLK, BLK), 0)
    t_pos = lax.broadcasted_iota(jnp.int32, (BLK, BLK), 1)
    visible = u_pos <= t_pos
    nb = SEG // BLK
    ks = [k_ref[pl.ds(i * BLK, BLK), :] for i in range(nb)]
    vs = [v_ref[pl.ds(i * BLK, BLK), :] for i in range(nb)]
    grad_k = [None] * nb
    grad_v = [None] * nb

    def plus(a, b):
        return b if a is None else a + b

    for tb in range(nb):
        q = q_ref[pl.ds(tb * BLK, BLK), :]
        lc = local_cot[tb * BLK : (tb + 1) * BLK]
        s = [mm(ks[u], q, NT) for u in range(tb + 1)]
        s[tb] = jnp.where(visible, s[tb], -1e30)
        top = functools.reduce(jnp.maximum, [jnp.max(a, axis=0, keepdims=True) for a in s])
        w = [jnp.exp2((a - top) * (SCALE * LOG2E)) for a in s]
        total = sum(jnp.sum(a, axis=0, keepdims=True) for a in w)
        inv = 1.0 / total
        p = [a * inv for a in w]
        gp = [mm(vs[u], lc, NT) for u in range(tb + 1)]
        inner = sum(jnp.sum(a * b, axis=0, keepdims=True) for a, b in zip(p, gp))
        gs = [(a * (b - inner) * SCALE).astype(BF16) for a, b in zip(p, gp)]
        gq_t = None
        for u in range(tb + 1):
            gq_t = plus(gq_t, mm(ks[u], gs[u], TN))
            grad_k[u] = plus(grad_k[u], mm(gs[u], q, NN))
            grad_v[u] = plus(grad_v[u], mm(p[u].astype(BF16), lc, NN))
        rows = pl.ds(tb * BLK, BLK)
        gq_ref[rows, :] = (gq_t.T + extra[tb * BLK : (tb + 1) * BLK]).astype(BF16)

    @pl.when(h == 0)
    def _():
        for u in range(nb):
            gk_ref[pl.ds(u * BLK, BLK), :] = grad_k[u]
            gv_ref[pl.ds(u * BLK, BLK), :] = grad_v[u]

    @pl.when(h > 0)
    def _():
        for u in range(nb):
            gk_ref[pl.ds(u * BLK, BLK), :] += grad_k[u]
            gv_ref[pl.ds(u * BLK, BLK), :] += grad_v[u]


def attention_call(seg, gates, qd, kv, kept, earlier=()):
    def head(first):
        return pl.BlockSpec((SEG, HD), lambda h: (seg, first + h))

    def shared(col):
        return pl.BlockSpec((SEG, HD), lambda h: (seg, col))

    return pl.pallas_call(
        attention_kernel,
        grid=(4,),
        in_specs=[
            pl.BlockSpec(memory_space=SMEM),
            head(0),
            head(4),
            shared(0),
            shared(1),
            pl.BlockSpec((HD, HD), lambda h: (4 * seg + h, 0)),
            pl.BlockSpec((8, HD), lambda h: (9 * HD // 8 + 4 * seg + h, 0)),
        ]
        + [pl.BlockSpec(memory_space=pl.ANY)] * len(earlier),
        out_specs=[head(0), shared(0), shared(0), pl.BlockSpec((8, HD), lambda h: (0, 0))],
        out_shape=(
            jax.ShapeDtypeStruct((2 * SEG, 6 * HD), BF16),
            jax.ShapeDtypeStruct((2 * SEG, HD), F32),
            jax.ShapeDtypeStruct((2 * SEG, HD), F32),
            jax.ShapeDtypeStruct((8, HD), F32),
        ),
        input_output_aliases={7 + i: i for i in range(len(earlier))},
        compiler_params=params(53),
        cost_estimate=cost(4 * 5 * 2 * SEG * SEG * HD, 3 << 20, 4 * SEG * SEG),
        name="attention",
    )(gates, qd, qd, kv, kv, kept, kept, *earlier)


def memory_kernel(
    core_ref, gate_ref, qd_ref, own_ref, other_ref, held_ref, held_other_ref,
    kept_ref, send_ref, rows_ref,
):
    later = None
    later_norm = None
    is_first = core_ref[0] == 0
    m0, t0 = term(other_ref, 0)
    m1, t1 = term(other_ref, 1)
    for h in range(4):
        cols = pl.ds(h * HD, HD)
        dcols = pl.ds((4 + h) * HD, HD)
        gate = gate_ref[h]
        here = is_first if h < 2 else jnp.logical_not(is_first)
        memory, norm, _ = (
            jnp.where(here, a, b)
            for a, b in zip(load_state(held_ref, h % 2), load_state(held_other_ref, h % 2))
        )
        fade = jnp.exp(-rate_row(other_ref, 1, h))
        both = jnp.exp(-(rate_row(other_ref, 0, h) + rate_row(other_ref, 1, h)))
        memory = jnp.where(is_first, memory, both * memory + (fade * m0 + m1))
        norm = jnp.where(is_first, norm, both * norm + (fade * t0 + t1))
        decay = jnp.exp(-rate_row(own_ref, 0, h))
        cots = []
        for e in range(2):
            if e == 1:
                moment, total = term(own_ref, 0)
                memory = decay * memory + moment
                norm = decay * norm + total
            rows = pl.ds(e * SEG, SEG)
            memory_low = memory.astype(BF16)
            kept_ref[pl.ds((4 * e + h) * HD, HD), :] = memory
            kept_ref[pl.ds(9 * HD + (4 * e + h) * 8, 8), :] = jnp.broadcast_to(norm, (8, HD))
            sq, _, num_cot, den_cot = retrieval_cots(
                gate, qd_ref[rows, cols], qd_ref[rows, dcols], memory_low, norm
            )
            state_cot = mm(sq.astype(BF16), num_cot.astype(BF16), TN)
            cots.append((state_cot, jnp.sum(sq * den_cot, axis=0, keepdims=True)))
        own = cots[0][0] + decay * cots[1][0]
        own_norm = cots[0][1] + decay * cots[1][1]
        rows_ref[:, 2 * h, :] = own[:HALF]
        rows_ref[:, 2 * h + 1, :] = own[HALF:]
        rows_ref[:, 8 + h, :] = jnp.broadcast_to(own_norm, (HALF, HD))
        later = cots[1][0] if later is None else later + cots[1][0]
        later_norm = cots[1][1] if later_norm is None else later_norm + cots[1][1]
    lane = lax.broadcasted_iota(jnp.int32, (1, HD), 1)
    rest = jnp.zeros((1, HD), F32)
    for e in range(2):
        for h in range(4):
            rest = jnp.where(lane == 4 * e + h, rate_row(own_ref, e, h), rest)
    for part in range(4):
        upper, rest = split_rows(rest)
        rows_ref[:, 12 + part, :] = jnp.broadcast_to(upper, (HALF, HD))
    send_ref[...] = rows_ref[...].astype(BF16)
    kept_ref[pl.ds(8 * HD, HD), :] = later
    kept_ref[pl.ds(9 * HD + 64, 8), :] = jnp.broadcast_to(later_norm, (8, HD))


def memory_call(core, gates, qd, own, other, held, held_other):
    return pl.pallas_call(
        memory_kernel,
        in_specs=[pl.BlockSpec(memory_space=SMEM)] * 2 + [pl.BlockSpec(memory_space=VMEM)] * 5,
        out_shape=(
            jax.ShapeDtypeStruct((9 * HD + 72, HD), F32),
            jax.ShapeDtypeStruct((HALF, 16, HD), BF16),
        ),
        scratch_shapes=[pltpu.VMEM((HALF, 16, HD), F32)],
        compiler_params=params(24),
        cost_estimate=cost(8 * 2 * 2 * SEG * HD * HD, 3 << 20, 8 * SEG * HD),
        name="memory",
    )(core, gates, qd, own, other, held, held_other)


def backward_kernel(me_ref, in_ref, earlier_ref, out_ref, norm_ref, rows_ref):
    del earlier_ref
    rows_ref[...] = in_ref[...].astype(F32)
    rates = sum(rows_ref[:, 12 + part, :] for part in range(3))
    c = cumulative(rates)
    after = c["cols"] > c["rows"]
    mine = lax.broadcasted_iota(jnp.int32, (HALF, HD), 0) == me_ref[0]
    one = zero = None
    for h in range(4):
        gap = pair_row(c["exc_row"], h) - pair_col(c["inc_col"], h)
        weight = jnp.exp(jnp.where(after, -gap, -1e30))
        own = jnp.concatenate(
            [rows_ref[:, 2 * h, :], rows_ref[:, 2 * h + 1, :], rows_ref[:, 8 + h, :]], axis=1
        )
        carried = mm(weight, own, NN, EXACT)
        earlier = jnp.exp(-rates[:, 4 + h : 5 + h]) * carried
        one = carried if one is None else one + carried
        zero = earlier if zero is None else zero + earlier
    for e, value in ((0, zero), (1, one)):
        out_ref[:, 2 * e, :] = value[:, :HD]
        out_ref[:, 2 * e + 1, :] = value[:, HD : 2 * HD]
        own = jnp.sum(jnp.where(mine, value[:, 2 * HD :], 0.0), axis=0, keepdims=True)
        norm_ref[4 * e : 4 * e + 4, :] = jnp.broadcast_to(own, (4, HD))


def backward_call(me, recv, earlier):
    return pl.pallas_call(
        backward_kernel,
        in_specs=[pl.BlockSpec(memory_space=SMEM)] + [
            pl.BlockSpec(memory_space=VMEM),
            pl.BlockSpec(memory_space=pl.ANY),
        ],
        out_shape=(
            jax.ShapeDtypeStruct((HALF, 4, HD), F32),
            jax.ShapeDtypeStruct((8, HD), F32),
        ),
        scratch_shapes=[pltpu.VMEM((HALF, 16, HD), F32)],
        compiler_params=params(16),
        cost_estimate=cost(4 * 2 * 64 * 64 * 384 * 6, 1 << 20, 4 * 4096),
        name="backward_scan",
    )(me, recv, earlier)


def finish_kernel(
    grads_ref, kv_ref, cot_ref, norm_ref, later_ref, later_norm_ref, gk_ref, gv_ref, out_ref
):
    del grads_ref
    is_last = pl.program_id(0) == 1

    def rows(low, high):
        return jnp.where(is_last, high, low)

    moment_cot = jnp.concatenate(
        [
            rows(cot_ref[:, 0, :], cot_ref[:, 2, :]),
            rows(cot_ref[:, 1, :], cot_ref[:, 3, :]),
        ],
        axis=0,
    )
    moment_cot = moment_cot + rows(later_ref[...], 0.0)
    total_cot = rows(norm_ref[0:1, :] + later_norm_ref[0:1, :], norm_ref[4:5, :])
    sk, slope = features_of(kv_ref[:, :HD].astype(F32))
    high, low = split(moment_cot)
    values = kv_ref[:, HD:]
    feat_cot = mm(values, high, NT) + mm(values, low, NT) + total_cot
    extra_v = mm3(sk, (high, low), NN)
    out_ref[:, :HD] = (gk_ref[...] + feat_cot * slope).astype(BF16)
    out_ref[:, HD:] = (gv_ref[...] + extra_v).astype(BF16)


def finish_call(grads, kv, cot, norm, kept, gk, gv):
    part = pl.BlockSpec((SEG, HD), lambda e: (e, 0))
    return pl.pallas_call(
        finish_kernel,
        grid=(2,),
        in_specs=[
            pl.BlockSpec(memory_space=pl.ANY),
            pl.BlockSpec((SEG, 2 * HD), lambda e: (e, 0)),
            pl.BlockSpec((HALF, 4, HD), lambda e: (0, 0, 0)),
            pl.BlockSpec((8, HD), lambda e: (0, 0)),
            pl.BlockSpec((HD, HD), lambda e: (8, 0)),
            pl.BlockSpec((8, HD), lambda e: (9 * HD // 8 + 8, 0)),
            part,
            part,
        ],
        out_specs=pl.BlockSpec((SEG, 2 * HD), lambda e: (e, 2)),
        out_shape=jax.ShapeDtypeStruct((2 * SEG, 6 * HD), BF16),
        input_output_aliases={0: 0},
        compiler_params=params(53),
        cost_estimate=cost(2 * 5 * 2 * SEG * HD * HD, 3 << 20, 2 * SEG * HD),
        name="finish",
    )(grads, kv, cot, norm, kept, kept, gk, gv)


def copies_kernel(moves, count, *refs):
    refs, sems = refs[:count], refs[count]
    copies = [
        pltpu.make_async_copy(refs[a].at[src], refs[b].at[dst], sems.at[i])
        for i, (a, src, b, dst) in enumerate(moves)
    ]
    for copy in copies:
        copy.start()
    for copy in copies:
        copy.wait()


def copies_call(moves, arrays, outs, mib, name):
    return pl.pallas_call(
        functools.partial(copies_kernel, moves, len(arrays) + len(outs)),
        in_specs=[pl.BlockSpec(memory_space=VMEM)] * len(arrays),
        out_specs=[pl.BlockSpec(memory_space=pl.ANY)] * len(outs),
        out_shape=[jax.ShapeDtypeStruct(shape, BF16) for shape in outs],
        scratch_shapes=[pltpu.SemaphoreType.DMA((len(moves),))],
        compiler_params=params(mib),
        cost_estimate=cost(0, 4 * sum(math.prod(shape) for shape in outs)),
        name=name,
    )(*arrays)


def pack_pair(x, y):
    tokens, width = x.shape[0], x.shape[1] // 8
    every = slice(None)
    moves = [
        (a, (every, pl.ds(g * width, width)), 2, (g, every, pl.ds(a * width, width)))
        for g in range(8)
        for a in range(2)
    ]
    return copies_call(moves, (x, y), [(8, tokens, 2 * width)], 60, "pack_pair")[0]


def unpack_grads(x):
    tokens = x.shape[1]
    every = slice(None)
    widths = (4 * HD, HD, HD)
    starts = (0, 4 * HD, 5 * HD)
    moves = [
        (0, (g, every, pl.ds(start, width)), 1 + i, (every, pl.ds(g * width, width)))
        for g in range(8)
        for i, (start, width) in enumerate(zip(starts, widths))
    ]
    outs = [(tokens, 8 * width) for width in widths]
    return copies_call(moves, (x,), outs, 8, "unpack_grads")


def side_by_side(x, y):
    tokens, width = x.shape[0], x.shape[1] // 8
    blocks = jnp.concatenate([a.reshape(tokens, 8, width) for a in (x, y)], axis=2)
    return jnp.transpose(blocks, (1, 0, 2))


def to_heads(blocks):
    moved = lax.all_to_all(blocks, "tp", split_axis=0, concat_axis=0, tiled=True)
    return moved.reshape(-1, blocks.shape[2])


def to_tokens(x):
    blocks = x.reshape(8, x.shape[0] // 8, x.shape[1])
    return lax.all_to_all(blocks, "tp", split_axis=0, concat_axis=0, tiled=True)


def over_seq(x):
    return lax.all_to_all(x, "seq", split_axis=0, concat_axis=0, tiled=True)


def local(query, keys, values, cotangent, rate, gate_logit):
    me = lax.axis_index("seq").astype(jnp.int32).reshape(1)
    core = me % 2
    gates = jax.nn.sigmoid(gate_logit)
    rate_rows = jnp.broadcast_to(rate.reshape(8, 1), (8, HD))
    kv = to_heads(pack_pair(keys, values))
    qd = to_heads(side_by_side(query, cotangent))
    own = moments_call(kv, rate_rows)
    other = swap_cores(own)
    base, send = chip_call(core, own, other)
    held = exclusive_scan(base, send, True)
    held_other = swap_cores(held)
    kept, cots = memory_call(core, gates, qd, own, other, held, held_other)
    arrived = over_seq(cots)
    *part, mark = attention_call(0, gates, qd, kv, kept)
    carried, carried_norm = backward_call(me, arrived, mark)
    cot = over_seq(carried)
    grads, gk, gv, _ = attention_call(1, gates, qd, kv, kept, part)
    grads = finish_call(grads, kv, cot, carried_norm, kept, gk, gv)
    return tuple(unpack_grads(to_tokens(grads)))


def solution(mesh):
    rows = P(("seq", "tp"), None)
    in_specs = (rows, rows, rows, rows, P("seq", "tp"), P("tp"))
    return jax.shard_map(
        local, mesh=mesh, in_specs=in_specs, out_specs=(rows, rows, rows), check_vma=False
    )
```
